128 devices in a mesh: ctx: 16 (over y, x_lo, core), dp: 8 (over x_hi, z).
Axes of the slice: x: 4 (x_hi: 2, x_lo: 2; x = x_hi * 2 + x_lo), y: 4, z: 4, core: 2. Of those that a mesh axis runs over, the one named last changes fastest.
Arguments:
- projected: bfloat16 [3, 4096, 4096], P(None, 'dp', 'ctx'), may hold values from -6 to 6
- filters: float32 [256, 4096], P(None, ('ctx', 'dp')), may hold values from -0.125 to 0.125
- cotangent: bfloat16 [4096, 4096], P('dp', 'ctx'), may hold values from -6 to 6
Outputs:
- mixed: bfloat16 [4096, 4096], P('dp', 'ctx')
- proj_grad: bfloat16 [3, 4096, 4096], P(None, 'dp', 'ctx')
- filter_grad: float32 [256, 4096], P(None, ('ctx', 'dp'))
The draws below stay inside these ranges and needn't reach their ends.
All inputs are finite; a program needn't handle non-finite values.
Results may differ from the reference program's by a relative error of at most 0.0017.
Values sent between devices are 32-bit elements; how exact they have to be, the bound alone decides.
A program may use at most 64 MiB of HBM per device.

```python
import jax
import jax.numpy as jnp

GROUP = 16
C = 4096
G = 256
SEQ_LEN = 4096


def block_scale(own_key, dims, cuts, least, top_value):
    factor_of, own = 1.0, jax.random.fold_in(own_key, 6)
    for dim, blocks in cuts:
        draws = jnp.exp(jax.random.uniform(jax.random.fold_in(own, dim), (blocks,), jnp.float32, least / len(cuts), top_value / len(cuts)))
        factor_of = factor_of * jnp.repeat(draws, dims[dim] // blocks).reshape([-1 if axis == dim else 1 for axis in range(len(dims))])
    return factor_of


def normal_values(own_key, dims, spread, most, pieces=(), dtype=jnp.bfloat16):
    level = block_scale(own_key, dims, pieces, -0.22, 0.18) if pieces else 1.0
    result = jax.random.normal(own_key, dims, jnp.float32) * spread * level
    return jnp.minimum(jnp.maximum(result, -most), most).astype(dtype)


def setup_inputs(seed: int = 0) -> dict:
    key_of = jax.random.split(jax.random.key(seed), 4)
    projected = normal_values(key_of[0], (3, C, SEQ_LEN), 1.0, 6.0, ((1, 8), (2, 16)))
    filters = normal_values(key_of[1], (G, SEQ_LEN), (SEQ_LEN // 2) ** -0.5, 0.125, ((1, 128),), jnp.float32)
    cotangent = normal_values(key_of[2], (C, SEQ_LEN), 1.0, 6.0, ((0, 8), (1, 16)))
    return dict(projected=projected, filters=filters, cotangent=cotangent)


def causal_part(spectrum, total):
    return jnp.fft.irfft(spectrum, n=2 * total)[..., :total]


def reference(projected, filters, cotangent):
    total = SEQ_LEN
    filter_spec = jnp.fft.rfft(filters, n=2 * total)[:, None, :]
    features = projected.astype(jnp.float32)
    gate_query = features[0]
    key_part = features[1]
    value_part = features[2]
    product = (key_part * value_part).reshape(G, GROUP, total)
    product_spec = jnp.fft.rfft(product, n=2 * total)
    conv = causal_part(product_spec * filter_spec, total).reshape(C, total)
    mixed = (gate_query * conv).astype(jnp.bfloat16)
    cot_values = cotangent.astype(jnp.float32)
    gate_grad = cot_values * conv
    conv_cot = (cot_values * gate_query).reshape(G, GROUP, total)
    cot_spec = jnp.fft.rfft(conv_cot, n=2 * total)
    product_grad = causal_part(jnp.conj(filter_spec) * cot_spec, total).reshape(C, total)
    filter_grad = jnp.sum(causal_part(jnp.conj(product_spec) * cot_spec, total), axis=1).astype(jnp.float32)
    proj_grad = jnp.stack([gate_grad, product_grad * value_part, product_grad * key_part]).astype(jnp.bfloat16)
    return mixed, proj_grad, filter_grad
```

```python
import functools

import jax
import jax.numpy as jnp
from jax import lax
from jax.experimental import pallas as pl
from jax.experimental.pallas import tpu as pltpu
from jax.sharding import PartitionSpec as P

MESH = pl.DeviceIdType.MESH
GROUP = 16
NC = 16
ND = 8
OWN = 2
BLK = 256
HALF = 128
F32 = jnp.float32
BF16 = jnp.bfloat16
NT = (((1,), (1,)), ((), ()))


def dot(left, right):
    return jnp.dot(left, right, preferred_element_type=F32)


def dot_nt(left, right):
    return lax.dot_general(left, right, NT, preferred_element_type=F32)


def split(value):
    high = value.astype(BF16)
    return high, (value - high.astype(F32)).astype(BF16)


def kernel(
    proj, filt, cot, mixed, pgrad, fgrad,
    sp, sq, rp, rq, yb, zb, cv, pv,
    fs, fd, ft, fr, hx, r1h, r1l,
    xh, xl, pth, ptl, qh, ql, s1, s2, fo, fa, fb, fc,
    ssem, rsem, dssem, drsem,
):
    me = lax.axis_index("ctx")
    dp = lax.axis_index("dp")

    def ctx_peer(o):
        return lax.rem(me + o, NC)

    def dp_peer(o):
        return lax.rem(dp + o, ND)

    def ctx_copy(kind, o, src, dst):
        return pltpu.make_async_remote_copy(
            src_ref=src, dst_ref=dst, send_sem=ssem.at[kind, o], recv_sem=rsem.at[kind, o],
            device_id=(ctx_peer(o), dp), device_id_type=MESH)

    def dp_copy(kind, o, src, dst):
        return pltpu.make_async_remote_copy(
            src_ref=src, dst_ref=dst, send_sem=dssem.at[kind, o], recv_sem=drsem.at[kind, o],
            device_id=(me, dp_peer(o)), device_id_type=MESH)

    def p_copy(o):
        return ctx_copy(0, o, sp.at[ctx_peer(o)], rp.at[:, me])

    def q_copy(o):
        return ctx_copy(1, o, sq.at[ctx_peer(o)], rq.at[:, me])

    def y_copy(g, o):
        return ctx_copy(2 + g, o, yb.at[g, ctx_peer(o)], cv.at[me, g])

    def z_copy(g, o):
        return ctx_copy(4 + g, o, zb.at[g, ctx_peer(o)], pv.at[me, g])

    def f_copy(o):
        return ctx_copy(6, o, ft.at[lax.div(ctx_peer(o), 2)], fr.at[me])

    def g_copy(o):
        return ctx_copy(7, o, fo.at[ctx_peer(o)], fa.at[me])

    def fd_copy(o):
        return dp_copy(0, o, fs.at[dp_peer(o)], fd.at[dp])

    def gd_copy(o):
        return dp_copy(1, o, fb.at[dp_peer(o)], fc.at[dp])

    def over(n, body):
        @pl.loop(1, n)
        def _(o):
            body(o)

    barrier = pltpu.get_barrier_semaphore()
    over(NC, lambda o: pl.semaphore_signal(
        barrier, inc=1, device_id=(ctx_peer(o), dp), device_id_type=MESH))
    over(ND, lambda o: pl.semaphore_signal(
        barrier, inc=1, device_id=(me, dp_peer(o)), device_id_type=MESH))

    fs[...] = jnp.concatenate(
        [filt[pl.ds(q, 64, stride=4), :] for q in range(4)], axis=1
    ).reshape(ND, 8, HALF)

    @pl.loop(0, NC)
    def _(k):
        rows = pl.ds(pl.multiple_of(k * 32, 32), 32)
        gate = proj[0, rows, :].astype(F32)
        prod = proj[1, rows, :].astype(F32) * proj[2, rows, :].astype(F32)
        ccot = cot[rows, :].astype(F32) * gate
        for g in range(OWN):
            for h in range(2):
                sp[k, g, h] = prod[g * 16 : g * 16 + 16, h * HALF : (h + 1) * HALF]
                sq[k, g, h] = ccot[g * 16 : g * 16 + 16, h * HALF : (h + 1) * HALF]

    pl.semaphore_wait(barrier, NC + ND - 2)
    over(ND, lambda o: fd_copy(o).start())
    over(NC, lambda o: p_copy(o).start())
    fd[dp] = fs[dp]
    for g in range(OWN):
        rp[g, me] = sp[me, g]
        rq[g, me] = sq[me, g]
    hx[...] = jnp.zeros_like(hx)
    qh[512:, :] = jnp.zeros((256, HALF), BF16)
    ql[512:, :] = jnp.zeros((256, HALF), BF16)
    over(ND, lambda o: fd_copy(o).wait_recv())
    for s in range(8):
        ft[s] = fd[:, s, :]
    over(NC, lambda o: f_copy(o).start())
    over(NC, lambda o: q_copy(o).start())
    fr[me] = ft[lax.div(me, 2)]
    over(NC, lambda o: f_copy(o).wait_recv())

    lane32 = lax.broadcasted_iota(jnp.int32, (32, HALF), 1)
    odd = lax.rem(me, 2)
    for g in range(OWN):
        total = jnp.zeros((32, HALF), F32)
        for j in range(4):
            part = jnp.concatenate([fr[k, j :: 4, :] for k in range(NC)], axis=0)
            turned = [pltpu.roll(part, (32 * (j - 2 * e - g)) % HALF, axis=1) for e in range(2)]
            part = jnp.where(odd == 1, turned[1], turned[0])
            total = jnp.where((lane32 >= 32 * j) & (lane32 < 32 * j + 32), part, total)
        hx[g, 8:40, :] = total

    row = lax.broadcasted_iota(jnp.int32, (HALF, HALF), 0)
    lane = lax.broadcasted_iota(jnp.int32, (HALF, HALF), 1)
    for g in range(OWN):
        @pl.loop(0, 33)
        def _(q):
            first = jnp.broadcast_to(hx[g, pl.ds(39 - q, 1), :], (HALF, HALF))
            second = jnp.broadcast_to(hx[g, pl.ds(38 - q, 1), :], (HALF, HALF))
            value = jnp.where(lane + row < HALF, first, second)
            high, low = split(pltpu.roll(value, 0, axis=1, stride=1, stride_axis=0))
            rows = pl.ds(pl.multiple_of(q * HALF, HALF), HALF)
            r1h[g, rows, :] = high
            r1l[g, rows, :] = low

    def tile(strip, g, d):
        start = 3968 - 256 * d
        return jnp.concatenate(
            [strip[g, start : start + BLK, :], strip[g, start - HALF : start - HALF + BLK, :]],
            axis=1)

    flip = (row + lane == HALF - 1).astype(BF16)

    over(NC, lambda o: p_copy(o).wait_recv())
    @pl.loop(0, OWN)
    def _(g):
        part_h, part_l = split(rp[g].reshape(512, HALF))
        pth[g] = dot_nt(flip, part_h).astype(BF16)
        ptl[g] = dot_nt(flip, part_l).astype(BF16)
        whole = jnp.concatenate(
            [rp[g, :, 0].reshape(BLK, HALF), rp[g, :, 1].reshape(BLK, HALF)], axis=1)
        xh[...], xl[...] = split(whole)
        for d in range(NC):
            n = (NC - d) * 16
            high, low = tile(r1h, g, d), tile(r1l, g, d)
            value = dot(xh[:n], high) + dot(xl[:n], high) + dot(xh[:n], low)
            value = value.reshape(NC - d, 16, BLK)
            if d == 0:
                yb[g] = value
            else:
                yb[g, d:] += value
        over(NC, lambda o: y_copy(g, o).start())
        cv[me, g] = yb[g, me]

    over(NC, lambda o: q_copy(o).wait_recv())
    @pl.loop(0, OWN)
    def _(g):
        whole = jnp.concatenate(
            [rq[g, :, 0].reshape(BLK, HALF), rq[g, :, 1].reshape(BLK, HALF)], axis=1)
        xh[...], xl[...] = split(whole)
        for d in range(NC):
            high, low = tile(r1h, g, d), tile(r1l, g, d)
            value = dot_nt(xh[d * 16 :], high) + dot_nt(xl[d * 16 :], high) + dot_nt(xh[d * 16 :], low)
            value = value.reshape(NC - d, 16, BLK)
            if d == 0:
                zb[g] = value
            else:
                zb[g, : NC - d] += value
        over(NC, lambda o: z_copy(g, o).start())
        pv[me, g] = zb[g, me]

    below = lane <= row
    fo[...] = jnp.zeros_like(fo)
    lane16 = lax.broadcasted_iota(jnp.int32, (32, HALF), 1)
    s2[...] = jnp.zeros_like(s2)
    for g in range(OWN):
        qh[:512, :], ql[:512, :] = split(rq[g].reshape(512, HALF))
        for e in range(16):
            depth = 512 if e < 8 else 256
            high, low = [
                jnp.concatenate([b[32 * e : 32 * e + depth, :], b[32 * e + 16 : 32 * e + 16 + depth, :]], axis=1)
                for b in (qh, ql)]
            left_h, left_l = pth[g, :, :depth], ptl[g, :, :depth]
            value = dot(left_h, high) + dot(left_l, high) + dot(left_h, low)
            for h in range(2):
                lag = 2 * e + h
                turned = pltpu.roll(value[:, h * HALF : (h + 1) * HALF], 1, axis=1, stride=1, stride_axis=0)
                s1[g, lag : lag + 1, :] = jnp.sum(jnp.where(below, turned, 0.0), axis=0, keepdims=True)
                if lag:
                    s2[g, lag - 1 : lag, :] = jnp.sum(jnp.where(below, 0.0, turned), axis=0, keepdims=True)
    sums = [s1[g] + s2[g] for g in range(OWN)]
    for j in range(4):
        total = jnp.zeros((32, HALF), F32)
        for g in range(OWN):
            for e in range(2):
                turned = pltpu.roll(sums[g], (32 * (2 * e + g - j)) % HALF, axis=1)
                start = 32 * (2 * e + g)
                mask = (lane16 >= start) & (lane16 < start + 32) & (odd == e)
                total = jnp.where(mask, turned, total)
        total = total.reshape(NC, 2, HALF)
        for h in range(2):
            fo[:, 4 * h + j, :] = total[:, h, :]
    over(NC, lambda o: g_copy(o).start())
    fa[me] = fo[me]

    for g in range(OWN):
        over(NC, lambda o: y_copy(g, o).wait_recv())

    @pl.loop(0, NC)
    def _(k):
        rows = pl.ds(pl.multiple_of(k * 32, 32), 32)
        conv = cv[k].reshape(32, BLK)
        mixed[rows, :] = (proj[0, rows, :].astype(F32) * conv).astype(BF16)
        pgrad[0, rows, :] = (cot[rows, :].astype(F32) * conv).astype(BF16)

    over(NC, lambda o: g_copy(o).wait_recv())
    for s in range(8):
        fb[:, s, :] = fa[2 * s] + fa[2 * s + 1]
    over(ND, lambda o: gd_copy(o).start())
    fc[dp] = fb[dp]

    for g in range(OWN):
        over(NC, lambda o: z_copy(g, o).wait_recv())

    @pl.loop(0, NC)
    def _(k):
        rows = pl.ds(pl.multiple_of(k * 32, 32), 32)
        grad = pv[k].reshape(32, BLK)
        pgrad[1, rows, :] = (grad * proj[2, rows, :].astype(F32)).astype(BF16)
        pgrad[2, rows, :] = (grad * proj[1, rows, :].astype(F32)).astype(BF16)

    over(ND, lambda o: gd_copy(o).wait_recv())
    last = fc[...].reshape(64, HALF)
    for q in range(4):
        fgrad[pl.ds(q, 64, stride=4), :] = last[:, 32 * q : 32 * q + 32]

    def finish(o):
        for make in (p_copy, q_copy, f_copy, g_copy):
            make(o).wait_send()
        for g in range(OWN):
            y_copy(g, o).wait_send()
            z_copy(g, o).wait_send()

    over(NC, finish)

    def finish_dp(o):
        fd_copy(o).wait_send()
        gd_copy(o).wait_send()

    over(ND, finish_dp)


def on_device(projected, filters, cotangent):
    rows, cols = cotangent.shape
    vmem = pl.BlockSpec(memory_space=pltpu.VMEM)
    f32 = lambda *shape: pltpu.VMEM(shape, F32)
    b16 = lambda *shape: pltpu.VMEM(shape, BF16)
    strip = (OWN, 33 * HALF, HALF)
    return pl.pallas_call(
        kernel,
        out_shape=(
            jax.ShapeDtypeStruct((rows, cols), BF16),
            jax.ShapeDtypeStruct((3, rows, cols), BF16),
            jax.ShapeDtypeStruct(filters.shape, F32),
        ),
        in_specs=[vmem] * 3,
        out_specs=(vmem,) * 3,
        scratch_shapes=[
            f32(NC, OWN, 2, GROUP, HALF), f32(NC, OWN, 2, GROUP, HALF),
            f32(OWN, NC, 2, GROUP, HALF), f32(OWN, NC, 2, GROUP, HALF),
            f32(OWN, NC, GROUP, BLK), f32(OWN, NC, GROUP, BLK),
            f32(NC, OWN, GROUP, BLK), f32(NC, OWN, GROUP, BLK),
            f32(ND, 8, HALF), f32(ND, 8, HALF), f32(8, ND, HALF), f32(NC, 8, HALF),
            f32(OWN, 40, HALF), b16(*strip), b16(*strip),
            b16(BLK, BLK), b16(BLK, BLK), b16(OWN, HALF, 512), b16(OWN, HALF, 512),
            b16(768, HALF), b16(768, HALF), f32(OWN, 32, HALF), f32(OWN, 32, HALF),
            f32(NC, ND, HALF), f32(NC, ND, HALF), f32(ND, 8, HALF), f32(ND, 8, HALF),
            pltpu.SemaphoreType.DMA((8, NC)), pltpu.SemaphoreType.DMA((8, NC)),
            pltpu.SemaphoreType.DMA((2, ND)), pltpu.SemaphoreType.DMA((2, ND)),
        ],
        compiler_params=pltpu.CompilerParams(
            collective_id=0, has_side_effects=True, vmem_limit_bytes=40 << 20),
    )(projected, filters, cotangent)


def solution(mesh):
    in_specs = (P(None, "dp", "ctx"), P(None, ("ctx", "dp")), P("dp", "ctx"))
    out_specs = (P("dp", "ctx"), P(None, "dp", "ctx"), P(None, ("ctx", "dp")))
    return jax.shard_map(
        on_device, mesh=mesh, in_specs=in_specs, out_specs=out_specs, check_vma=False
    )
```

```python
import functools

import jax
import jax.numpy as jnp
from jax import lax
from jax.experimental import pallas as pl
from jax.experimental.pallas import tpu as pltpu
from jax.sharding import PartitionSpec as P

MESH = pl.DeviceIdType.MESH
GROUP = 16
NC = 16
ND = 8
OWN = 2
BLK = 256
HALF = 128
F32 = jnp.float32
BF16 = jnp.bfloat16
NT = (((1,), (1,)), ((), ()))


def dot(left, right):
    return jnp.dot(left, right, preferred_element_type=F32)


def dot_nt(left, right):
    return lax.dot_general(left, right, NT, preferred_element_type=F32)


def split(value):
    high = value.astype(BF16)
    return high, (value - high.astype(F32)).astype(BF16)


def kernel(
    proj_in, filt_in, cot_in, mixed, pgrad, fgrad,
    proj, filt, cot, filt_rows,
    sp, sq, rp, rq, yb, zb, cv, pv,
    fs, fd, ft, fr, hx, r1h, r1l,
    xh, xl, pth, ptl, qh, ql, s1, s2, fo, fa, fb, fc,
    ssem, rsem, dssem, drsem, lsem,
):
    me = lax.axis_index("ctx")
    dp = lax.axis_index("dp")

    def ctx_peer(o):
        return lax.rem(me + o, NC)

    def dp_peer(o):
        return lax.rem(dp + o, ND)

    def ctx_copy(kind, o, src, dst):
        return pltpu.make_async_remote_copy(
            src_ref=src, dst_ref=dst, send_sem=ssem.at[kind, o], recv_sem=rsem.at[kind, o],
            device_id=(ctx_peer(o), dp), device_id_type=MESH)

    def dp_copy(kind, o, src, dst):
        return pltpu.make_async_remote_copy(
            src_ref=src, dst_ref=dst, send_sem=dssem.at[kind, o], recv_sem=drsem.at[kind, o],
            device_id=(me, dp_peer(o)), device_id_type=MESH)

    def p_copy(o):
        return ctx_copy(0, o, sp.at[ctx_peer(o)], rp.at[:, me])

    def q_copy(o):
        return ctx_copy(1, o, sq.at[ctx_peer(o)], rq.at[:, me])

    def y_copy(g, o):
        return ctx_copy(2 + g, o, yb.at[g, ctx_peer(o)], cv.at[me, g])

    def z_copy(g, o):
        return ctx_copy(4 + g, o, zb.at[g, ctx_peer(o)], pv.at[me, g])

    def f_copy(o):
        return ctx_copy(6, o, ft.at[lax.div(ctx_peer(o), 2)], fr.at[me])

    def g_copy(o):
        return ctx_copy(7, o, fo.at[ctx_peer(o)], fa.at[me])

    def fd_copy(o):
        return dp_copy(0, o, fs.at[dp_peer(o)], fd.at[dp])

    def gd_copy(o):
        return dp_copy(1, o, fb.at[dp_peer(o)], fc.at[dp])

    def over(n, body):
        @pl.loop(1, n)
        def _(o):
            body(o)

    barrier = pltpu.get_barrier_semaphore()
    over(ND, lambda o: pl.semaphore_signal(
        barrier, inc=1, device_id=(me, dp_peer(o)), device_id_type=MESH))
    over(NC, lambda o: pl.semaphore_signal(
        barrier, inc=1, device_id=(ctx_peer(o), dp), device_id_type=MESH))
    loads = [
        pltpu.make_async_copy(filt_in, filt, lsem.at[0]),
        pltpu.make_async_copy(proj_in, proj, lsem.at[1]),
        pltpu.make_async_copy(cot_in, cot, lsem.at[2]),
    ]
    for load in loads:
        load.start()
    hx[...] = jnp.zeros_like(hx)
    qh[512:, :] = jnp.zeros((256, HALF), BF16)
    ql[512:, :] = jnp.zeros((256, HALF), BF16)
    fo[...] = jnp.zeros_like(fo)
    s2[...] = jnp.zeros_like(s2)
    loads[0].wait()
    filt_rows[...] = filt[...].T

    fs[...] = jnp.concatenate(
        [filt_rows[pl.ds(q, 64, stride=4), :] for q in range(4)], axis=1
    ).reshape(ND, 8, HALF)

    loads[1].wait()
    loads[2].wait()

    @pl.loop(0, NC, unroll=4)
    def _(k):
        rows = pl.ds(pl.multiple_of(k * 32, 32), 32)
        gate = proj[0, rows, :].astype(F32)
        prod = proj[1, rows, :].astype(F32) * proj[2, rows, :].astype(F32)
        ccot = cot[rows, :].astype(F32) * gate
        for g in range(OWN):
            for h in range(2):
                sp[k, g, h] = prod[g * 16 : g * 16 + 16, h * HALF : (h + 1) * HALF]
                sq[k, g, h] = ccot[g * 16 : g * 16 + 16, h * HALF : (h + 1) * HALF]

    pl.semaphore_wait(barrier, NC + ND - 2)
    over(ND, lambda o: fd_copy(o).start())
    over(NC, lambda o: p_copy(o).start())
    fd[dp] = fs[dp]
    for g in range(OWN):
        rp[g, me] = sp[me, g]
        rq[g, me] = sq[me, g]
    over(ND, lambda o: fd_copy(o).wait_recv())
    for s in range(8):
        ft[s] = fd[:, s, :]
    over(NC, lambda o: f_copy(o).start())
    over(NC, lambda o: q_copy(o).start())
    fr[me] = ft[lax.div(me, 2)]
    over(NC, lambda o: f_copy(o).wait_recv())

    lane32 = lax.broadcasted_iota(jnp.int32, (32, HALF), 1)
    odd = lax.rem(me, 2)
    for g in range(OWN):
        total = jnp.zeros((32, HALF), F32)
        for j in range(4):
            part = jnp.concatenate([fr[k, j :: 4, :] for k in range(NC)], axis=0)
            turned = [pltpu.roll(part, (32 * (j - 2 * e - g)) % HALF, axis=1) for e in range(2)]
            part = jnp.where(odd == 1, turned[1], turned[0])
            total = jnp.where((lane32 >= 32 * j) & (lane32 < 32 * j + 32), part, total)
        hx[g, 8:40, :] = total

    row = lax.broadcasted_iota(jnp.int32, (HALF, HALF), 0)
    lane = lax.broadcasted_iota(jnp.int32, (HALF, HALF), 1)

    def build(g):
        for q in range(32):
            first = jnp.broadcast_to(hx[g, 39 - q : 40 - q, :], (HALF, HALF))
            second = jnp.broadcast_to(hx[g, 38 - q : 39 - q, :], (HALF, HALF))
            value = jnp.where(lane + row < HALF, first, second)
            high, low = split(pltpu.roll(value, 0, axis=1, stride=1, stride_axis=0))
            r1h[g, q * HALF : (q + 1) * HALF, :] = high
            r1l[g, q * HALF : (q + 1) * HALF, :] = low
        r1h[g, 32 * HALF :, :] = jnp.zeros((HALF, HALF), BF16)
        r1l[g, 32 * HALF :, :] = jnp.zeros((HALF, HALF), BF16)

    def tile(strip, g, d):
        start = 3968 - 256 * d
        return jnp.concatenate(
            [strip[g, start : start + BLK, :], strip[g, start - HALF : start - HALF + BLK, :]],
            axis=1)

    flip = (row + lane == HALF - 1).astype(BF16)

    over(NC, lambda o: p_copy(o).wait_recv())
    @pl.loop(0, OWN)
    def _(g):
        build(g)
        whole = jnp.concatenate(
            [rp[g, :, 0].reshape(BLK, HALF), rp[g, :, 1].reshape(BLK, HALF)], axis=1)
        xh[...], xl[...] = split(whole)
        for d in range(NC):
            n = (NC - d) * 16
            high, low = tile(r1h, g, d), tile(r1l, g, d)
            both = dot(jnp.concatenate([xh[:n], xl[:n]], axis=0), high)
            value = both[:n] + both[n:] + dot(xh[:n], low)
            value = value.reshape(NC - d, 16, BLK)
            if d == 0:
                yb[g] = value
            else:
                yb[g, d:] += value
        over(NC, lambda o: y_copy(g, o).start())
        cv[me, g] = yb[g, me]

    @pl.loop(0, OWN)
    def _(g):
        part_h, part_l = split(rp[g].reshape(512, HALF))
        pth[g] = dot_nt(flip, part_h).astype(BF16)
        ptl[g] = dot_nt(flip, part_l).astype(BF16)

    over(NC, lambda o: q_copy(o).wait_recv())
    below = lane <= row
    lane16 = lax.broadcasted_iota(jnp.int32, (32, HALF), 1)
    for g in range(OWN):
        qh[:512, :], ql[:512, :] = split(rq[g].reshape(512, HALF))
        for e in range(16):
            depth = 512 if e < 8 else 256
            high, low = [
                jnp.concatenate([b[32 * e : 32 * e + depth, :], b[32 * e + 16 : 32 * e + 16 + depth, :]], axis=1)
                for b in (qh, ql)]
            left_h, left_l = pth[g, :, :depth], ptl[g, :, :depth]
            value = dot(left_h, high) + dot(left_l, high) + dot(left_h, low)
            for h in range(2):
                lag = 2 * e + h
                turned = pltpu.roll(value[:, h * HALF : (h + 1) * HALF], 1, axis=1, stride=1, stride_axis=0)
                s1[g, lag : lag + 1, :] = jnp.sum(jnp.where(below, turned, 0.0), axis=0, keepdims=True)
                if lag:
                    s2[g, lag - 1 : lag, :] = jnp.sum(jnp.where(below, 0.0, turned), axis=0, keepdims=True)
    sums = [s1[g] + s2[g] for g in range(OWN)]
    for j in range(4):
        total = jnp.zeros((32, HALF), F32)
        for g in range(OWN):
            for e in range(2):
                turned = pltpu.roll(sums[g], (32 * (2 * e + g - j)) % HALF, axis=1)
                start = 32 * (2 * e + g)
                mask = (lane16 >= start) & (lane16 < start + 32) & (odd == e)
                total = jnp.where(mask, turned, total)
        total = total.reshape(NC, 2, HALF)
        for h in range(2):
            fo[:, 4 * h + j, :] = total[:, h, :]
    over(NC, lambda o: g_copy(o).start())
    fa[me] = fo[me]

    @pl.loop(0, OWN)
    def _(g):
        whole = jnp.concatenate(
            [rq[g, :, 0].reshape(BLK, HALF), rq[g, :, 1].reshape(BLK, HALF)], axis=1)
        xh[...], xl[...] = split(whole)
        for d in range(NC):
            n = (NC - d) * 16
            high, low = tile(r1h, g, d), tile(r1l, g, d)
            both = dot_nt(jnp.concatenate([xh[d * 16 :], xl[d * 16 :]], axis=0), high)
            value = both[:n] + both[n:] + dot_nt(xh[d * 16 :], low)
            value = value.reshape(NC - d, 16, BLK)
            if d == 0:
                zb[g] = value
            else:
                zb[g, : NC - d] += value
        over(NC, lambda o: z_copy(g, o).start())
        pv[me, g] = zb[g, me]

    over(NC, lambda o: g_copy(o).wait_recv())
    for s in range(8):
        fb[:, s, :] = fa[2 * s] + fa[2 * s + 1]
    over(ND, lambda o: gd_copy(o).start())
    fc[dp] = fb[dp]

    def gate_block(k):
        rows = pl.ds(pl.multiple_of(k * 32, 32), 32)
        conv = cv[k].reshape(32, BLK)
        mixed[rows, :] = (proj[0, rows, :].astype(F32) * conv).astype(BF16)
        pgrad[0, rows, :] = (cot[rows, :].astype(F32) * conv).astype(BF16)

    def value_block(k):
        rows = pl.ds(pl.multiple_of(k * 32, 32), 32)
        grad = pv[k].reshape(32, BLK)
        pgrad[1, rows, :] = (grad * proj[2, rows, :].astype(F32)).astype(BF16)
        pgrad[2, rows, :] = (grad * proj[1, rows, :].astype(F32)).astype(BF16)

    def ctx_source(o):
        return lax.rem(me + NC - o, NC)

    gate_block(me)

    def take_conv(o):
        for g in range(OWN):
            y_copy(g, o).wait_recv()
        gate_block(ctx_source(o))

    over(NC, take_conv)
    value_block(me)

    def take_grad(o):
        for g in range(OWN):
            z_copy(g, o).wait_recv()
        value_block(ctx_source(o))

    over(NC, take_grad)

    over(ND, lambda o: gd_copy(o).wait_recv())
    last = fc[...].reshape(64, HALF)
    for q in range(4):
        filt_rows[pl.ds(q, 64, stride=4), :] = last[:, 32 * q : 32 * q + 32]
    fgrad[...] = filt_rows[...].T

    def finish(o):
        for make in (p_copy, q_copy, f_copy, g_copy):
            make(o).wait_send()
        for g in range(OWN):
            y_copy(g, o).wait_send()
            z_copy(g, o).wait_send()

    over(NC, finish)

    def finish_dp(o):
        fd_copy(o).wait_send()
        gd_copy(o).wait_send()

    over(ND, finish_dp)


def on_device(projected, filters, cotangent):
    rows, cols = cotangent.shape
    vmem = pl.BlockSpec(memory_space=pltpu.VMEM)
    f32 = lambda *shape: pltpu.VMEM(shape, F32)
    b16 = lambda *shape: pltpu.VMEM(shape, BF16)
    strip = (OWN, 33 * HALF, HALF)
    whole = pl.BlockSpec(memory_space=pl.ANY)
    mixed, proj_grad, filter_grad = pl.pallas_call(
        kernel,
        out_shape=(
            jax.ShapeDtypeStruct((rows, cols), BF16),
            jax.ShapeDtypeStruct((3, rows, cols), BF16),
            jax.ShapeDtypeStruct(filters.shape[::-1], F32),
        ),
        in_specs=[whole] * 3,
        out_specs=(vmem,) * 3,
        scratch_shapes=[
            b16(3, rows, cols), f32(*filters.shape[::-1]), b16(rows, cols), f32(*filters.shape),
            f32(NC, OWN, 2, GROUP, HALF), f32(NC, OWN, 2, GROUP, HALF),
            f32(OWN, NC, 2, GROUP, HALF), f32(OWN, NC, 2, GROUP, HALF),
            f32(OWN, NC, GROUP, BLK), f32(OWN, NC, GROUP, BLK),
            f32(NC, OWN, GROUP, BLK), f32(NC, OWN, GROUP, BLK),
            f32(ND, 8, HALF), f32(ND, 8, HALF), f32(8, ND, HALF), f32(NC, 8, HALF),
            f32(OWN, 40, HALF), b16(*strip), b16(*strip),
            b16(BLK, BLK), b16(BLK, BLK), b16(OWN, HALF, 512), b16(OWN, HALF, 512),
            b16(768, HALF), b16(768, HALF), f32(OWN, 32, HALF), f32(OWN, 32, HALF),
            f32(NC, ND, HALF), f32(NC, ND, HALF), f32(ND, 8, HALF), f32(ND, 8, HALF),
            pltpu.SemaphoreType.DMA((8, NC)), pltpu.SemaphoreType.DMA((8, NC)),
            pltpu.SemaphoreType.DMA((2, ND)), pltpu.SemaphoreType.DMA((2, ND)), pltpu.SemaphoreType.DMA((3,)),
        ],
        compiler_params=pltpu.CompilerParams(
            collective_id=0, has_side_effects=True, vmem_limit_bytes=56 << 20),
    )(projected, filters.T, cotangent)
    return mixed, proj_grad, filter_grad.T


def solution(mesh):
    in_specs = (P(None, "dp", "ctx"), P(None, ("ctx", "dp")), P("dp", "ctx"))
    out_specs = (P("dp", "ctx"), P(None, "dp", "ctx"), P(None, ("ctx", "dp")))
    return jax.shard_map(
        on_device, mesh=mesh, in_specs=in_specs, out_specs=out_specs, check_vma=False
    )
```

```python
import functools

import jax
import jax.numpy as jnp
from jax import lax
from jax.experimental import pallas as pl
from jax.experimental.pallas import tpu as pltpu
from jax.sharding import PartitionSpec as P

MESH = pl.DeviceIdType.MESH
GROUP = 16
NC = 16
ND = 8
OWN = 2
BLK = 256
HALF = 128
F32 = jnp.float32
BF16 = jnp.bfloat16
NT = (((1,), (1,)), ((), ()))


def dot(left, right):
    return jnp.dot(left, right, preferred_element_type=F32)


def dot_nt(left, right):
    return lax.dot_general(left, right, NT, preferred_element_type=F32)


def split(value):
    high = value.astype(BF16)
    return high, (value - high.astype(F32)).astype(BF16)


def kernel(
    proj_in, filt_in, cot_in, mixed, pgrad, fgrad,
    proj, filt, cot, filt_rows,
    sp, sq, rp, rq, yb, zb, cv, pv,
    fs, fd, ft, fr, hx, r1h, r1l,
    xh, xl, pth, ptl, qh, ql, s1, s2, fo, fa, fb, fc,
    ssem, rsem, lsem,
):
    me = lax.axis_index("ctx")
    dp = lax.axis_index("dp")

    def ctx_peer(o):
        return lax.rem(me + o, NC)

    def dp_peer(o):
        return lax.rem(dp + o, ND)

    def ctx_copy(kind, o, src, dst):
        return pltpu.make_async_remote_copy(
            src_ref=src, dst_ref=dst, send_sem=ssem.at[kind], recv_sem=rsem.at[kind],
            device_id=(ctx_peer(o), dp), device_id_type=MESH)

    def dp_copy(kind, o, src, dst):
        return pltpu.make_async_remote_copy(
            src_ref=src, dst_ref=dst, send_sem=ssem.at[8 + kind], recv_sem=rsem.at[8 + kind],
            device_id=(me, dp_peer(o)), device_id_type=MESH)

    def p_copy(o):
        return ctx_copy(0, o, sp.at[ctx_peer(o)], rp.at[:, me])

    def q_copy(o):
        return ctx_copy(1, o, sq.at[ctx_peer(o)], rq.at[:, me])

    def y_copy(g, o):
        return ctx_copy(2 + g, o, yb.at[g, ctx_peer(o)], cv.at[me, g])

    def z_copy(g, o):
        return ctx_copy(4 + g, o, zb.at[g, ctx_peer(o)], pv.at[me, g])

    def f_copy(o):
        return ctx_copy(6, o, ft.at[lax.div(ctx_peer(o), 2)], fr.at[me])

    def g_copy(o):
        return ctx_copy(7, o, fo.at[ctx_peer(o)], fa.at[me])

    def fd_copy(o):
        return dp_copy(0, o, fs.at[dp_peer(o)], fd.at[dp])

    def gd_copy(o):
        return dp_copy(1, o, fb.at[dp_peer(o)], fc.at[dp])

    totals = [
        rp.at[:, pl.ds(0, NC - 1)], rq.at[:, pl.ds(0, NC - 1)],
        cv.at[pl.ds(0, NC - 1), 0], cv.at[pl.ds(0, NC - 1), 1],
        pv.at[pl.ds(0, NC - 1), 0], pv.at[pl.ds(0, NC - 1), 1],
        fr.at[pl.ds(0, NC - 1)], fa.at[pl.ds(0, NC - 1)],
        fd.at[pl.ds(0, ND - 1)], fc.at[pl.ds(0, ND - 1)],
    ]

    def arrived(kind):
        pltpu.make_async_copy(totals[kind], totals[kind], rsem.at[kind]).wait()

    def sent(kind):
        pltpu.make_async_copy(totals[kind], totals[kind], ssem.at[kind]).wait()

    def over(n, body):
        @pl.loop(1, n)
        def _(o):
            body(o)

    barrier = pltpu.get_barrier_semaphore()
    over(ND, lambda o: pl.semaphore_signal(
        barrier, inc=1, device_id=(me, dp_peer(o)), device_id_type=MESH))
    over(NC, lambda o: pl.semaphore_signal(
        barrier, inc=1, device_id=(ctx_peer(o), dp), device_id_type=MESH))
    loads = [
        pltpu.make_async_copy(filt_in, filt, lsem.at[0]),
        pltpu.make_async_copy(proj_in, proj, lsem.at[1]),
        pltpu.make_async_copy(cot_in, cot, lsem.at[2]),
    ]
    for load in loads:
        load.start()
    hx[...] = jnp.zeros_like(hx)
    qh[512:, :] = jnp.zeros((256, HALF), BF16)
    ql[512:, :] = jnp.zeros((256, HALF), BF16)
    fo[...] = jnp.zeros_like(fo)
    s2[...] = jnp.zeros_like(s2)
    loads[0].wait()
    filt_rows[...] = filt[...].T

    fs[...] = jnp.concatenate(
        [filt_rows[pl.ds(q, 64, stride=4), :] for q in range(4)], axis=1
    ).reshape(ND, 8, HALF)

    loads[1].wait()
    loads[2].wait()

    @pl.loop(0, NC, unroll=4)
    def _(k):
        rows = pl.ds(pl.multiple_of(k * 32, 32), 32)
        gate = proj[0, rows, :].astype(F32)
        prod = proj[1, rows, :].astype(F32) * proj[2, rows, :].astype(F32)
        ccot = cot[rows, :].astype(F32) * gate
        for g in range(OWN):
            for h in range(2):
                sp[k, g, h] = prod[g * 16 : g * 16 + 16, h * HALF : (h + 1) * HALF]
                sq[k, g, h] = ccot[g * 16 : g * 16 + 16, h * HALF : (h + 1) * HALF]

    pl.semaphore_wait(barrier, NC + ND - 2)
    over(ND, lambda o: fd_copy(o).start())
    over(NC, lambda o: p_copy(o).start())
    fd[dp] = fs[dp]
    for g in range(OWN):
        rp[g, me] = sp[me, g]
        rq[g, me] = sq[me, g]
    arrived(8)
    for s in range(8):
        ft[s] = fd[:, s, :]
    over(NC, lambda o: f_copy(o).start())
    over(NC, lambda o: q_copy(o).start())
    fr[me] = ft[lax.div(me, 2)]
    arrived(6)

    lane32 = lax.broadcasted_iota(jnp.int32, (32, HALF), 1)
    odd = lax.rem(me, 2)
    for g in range(OWN):
        total = jnp.zeros((32, HALF), F32)
        for j in range(4):
            part = jnp.concatenate([fr[k, j :: 4, :] for k in range(NC)], axis=0)
            turned = [pltpu.roll(part, (32 * (j - 2 * e - g)) % HALF, axis=1) for e in range(2)]
            part = jnp.where(odd == 1, turned[1], turned[0])
            total = jnp.where((lane32 >= 32 * j) & (lane32 < 32 * j + 32), part, total)
        hx[g, 8:40, :] = total

    row = lax.broadcasted_iota(jnp.int32, (HALF, HALF), 0)
    lane = lax.broadcasted_iota(jnp.int32, (HALF, HALF), 1)

    def build(g):
        for q in range(32):
            first = jnp.broadcast_to(hx[g, 39 - q : 40 - q, :], (HALF, HALF))
            second = jnp.broadcast_to(hx[g, 38 - q : 39 - q, :], (HALF, HALF))
            value = jnp.where(lane + row < HALF, first, second)
            high, low = split(pltpu.roll(value, 0, axis=1, stride=1, stride_axis=0))
            r1h[g, q * HALF : (q + 1) * HALF, :] = high
            r1l[g, q * HALF : (q + 1) * HALF, :] = low
        r1h[g, 32 * HALF :, :] = jnp.zeros((HALF, HALF), BF16)
        r1l[g, 32 * HALF :, :] = jnp.zeros((HALF, HALF), BF16)

    def tile(strip, g, d):
        start = 3968 - 256 * d
        return jnp.concatenate(
            [strip[g, start : start + BLK, :], strip[g, start - HALF : start - HALF + BLK, :]],
            axis=1)

    flip = (row + lane == HALF - 1).astype(BF16)

    arrived(0)
    @pl.loop(0, OWN)
    def _(g):
        build(g)
        whole = jnp.concatenate(
            [rp[g, :, 0].reshape(BLK, HALF), rp[g, :, 1].reshape(BLK, HALF)], axis=1)
        xh[...], xl[...] = split(whole)
        for d in range(NC):
            n = (NC - d) * 16
            high, low = tile(r1h, g, d), tile(r1l, g, d)
            both = dot(jnp.concatenate([xh[:n], xl[:n]], axis=0), high)
            value = both[:n] + both[n:] + dot(xh[:n], low)
            value = value.reshape(NC - d, 16, BLK)
            if d == 0:
                yb[g] = value
            else:
                yb[g, d:] += value
        over(NC, lambda o: y_copy(g, o).start())
        cv[me, g] = yb[g, me]

    @pl.loop(0, OWN)
    def _(g):
        part_h, part_l = split(rp[g].reshape(512, HALF))
        pth[g] = dot_nt(flip, part_h).astype(BF16)
        ptl[g] = dot_nt(flip, part_l).astype(BF16)

    arrived(1)
    below = lane <= row
    lane16 = lax.broadcasted_iota(jnp.int32, (32, HALF), 1)
    for g in range(OWN):
        qh[:512, :], ql[:512, :] = split(rq[g].reshape(512, HALF))
        for e in range(16):
            depth = 512 if e < 8 else 256
            high, low = [
                jnp.concatenate([b[32 * e : 32 * e + depth, :], b[32 * e + 16 : 32 * e + 16 + depth, :]], axis=1)
                for b in (qh, ql)]
            left_h, left_l = pth[g, :, :depth], ptl[g, :, :depth]
            value = dot(left_h, high) + dot(left_l, high) + dot(left_h, low)
            for h in range(2):
                lag = 2 * e + h
                turned = pltpu.roll(value[:, h * HALF : (h + 1) * HALF], 1, axis=1, stride=1, stride_axis=0)
                s1[g, lag : lag + 1, :] = jnp.sum(jnp.where(below, turned, 0.0), axis=0, keepdims=True)
                if lag:
                    s2[g, lag - 1 : lag, :] = jnp.sum(jnp.where(below, 0.0, turned), axis=0, keepdims=True)
    sums = [s1[g] + s2[g] for g in range(OWN)]
    for j in range(4):
        total = jnp.zeros((32, HALF), F32)
        for g in range(OWN):
            for e in range(2):
                turned = pltpu.roll(sums[g], (32 * (2 * e + g - j)) % HALF, axis=1)
                start = 32 * (2 * e + g)
                mask = (lane16 >= start) & (lane16 < start + 32) & (odd == e)
                total = jnp.where(mask, turned, total)
        total = total.reshape(NC, 2, HALF)
        for h in range(2):
            fo[:, 4 * h + j, :] = total[:, h, :]
    over(NC, lambda o: g_copy(o).start())
    fa[me] = fo[me]

    @pl.loop(0, OWN)
    def _(g):
        whole = jnp.concatenate(
            [rq[g, :, 0].reshape(BLK, HALF), rq[g, :, 1].reshape(BLK, HALF)], axis=1)
        xh[...], xl[...] = split(whole)
        for d in range(NC):
            n = (NC - d) * 16
            high, low = tile(r1h, g, d), tile(r1l, g, d)
            both = dot_nt(jnp.concatenate([xh[d * 16 :], xl[d * 16 :]], axis=0), high)
            value = both[:n] + both[n:] + dot_nt(xh[d * 16 :], low)
            value = value.reshape(NC - d, 16, BLK)
            if d == 0:
                zb[g] = value
            else:
                zb[g, : NC - d] += value
        over(NC, lambda o: z_copy(g, o).start())
        pv[me, g] = zb[g, me]

    arrived(7)
    for s in range(8):
        fb[:, s, :] = fa[2 * s] + fa[2 * s + 1]
    over(ND, lambda o: gd_copy(o).start())
    fc[dp] = fb[dp]

    arrived(2)
    arrived(3)

    @pl.loop(0, NC, unroll=4)
    def _(k):
        rows = pl.ds(pl.multiple_of(k * 32, 32), 32)
        conv = cv[k].reshape(32, BLK)
        mixed[rows, :] = (proj[0, rows, :].astype(F32) * conv).astype(BF16)
        pgrad[0, rows, :] = (cot[rows, :].astype(F32) * conv).astype(BF16)

    for g in range(OWN):
        arrived(4 + g)

        @pl.loop(0, NC, unroll=4)
        def _(k):
            rows = pl.ds(pl.multiple_of(k * 32 + g * 16, 16), 16)
            grad = pv[k, g]
            pgrad[1, rows, :] = (grad * proj[2, rows, :].astype(F32)).astype(BF16)
            pgrad[2, rows, :] = (grad * proj[1, rows, :].astype(F32)).astype(BF16)

    arrived(9)
    last = fc[...].reshape(64, HALF)
    for q in range(4):
        filt_rows[pl.ds(q, 64, stride=4), :] = last[:, 32 * q : 32 * q + 32]
    fgrad[...] = filt_rows[...].T

    for kind in range(10):
        sent(kind)


def write_out(mixed, pgrad, fgrad, mixed_out, pgrad_out, fgrad_out, sem):
    pairs = [(mixed, mixed_out), (pgrad, pgrad_out), (fgrad, fgrad_out)]
    copies = [pltpu.make_async_copy(a, b, sem.at[i]) for i, (a, b) in enumerate(pairs)]
    for copy in copies:
        copy.start()
    for copy in copies:
        copy.wait()


def on_device(projected, filters, cotangent):
    rows, cols = cotangent.shape
    vmem = pl.BlockSpec(memory_space=pltpu.VMEM)
    f32 = lambda *shape: pltpu.VMEM(shape, F32)
    b16 = lambda *shape: pltpu.VMEM(shape, BF16)
    strip = (OWN, 33 * HALF, HALF)
    whole = pl.BlockSpec(memory_space=pltpu.HBM)
    mixed, proj_grad, filter_grad = pl.pallas_call(
        kernel,
        out_shape=(
            jax.ShapeDtypeStruct((rows, cols), BF16),
            jax.ShapeDtypeStruct((3, rows, cols), BF16),
            jax.ShapeDtypeStruct(filters.shape[::-1], F32),
        ),
        in_specs=[whole] * 3,
        out_specs=(vmem,) * 3,
        scratch_shapes=[
            b16(3, rows, cols), f32(*filters.shape[::-1]), b16(rows, cols), f32(*filters.shape),
            f32(NC, OWN, 2, GROUP, HALF), f32(NC, OWN, 2, GROUP, HALF),
            f32(OWN, NC, 2, GROUP, HALF), f32(OWN, NC, 2, GROUP, HALF),
            f32(OWN, NC, GROUP, BLK), f32(OWN, NC, GROUP, BLK),
            f32(NC, OWN, GROUP, BLK), f32(NC, OWN, GROUP, BLK),
            f32(ND, 8, HALF), f32(ND, 8, HALF), f32(8, ND, HALF), f32(NC, 8, HALF),
            f32(OWN, 40, HALF), b16(*strip), b16(*strip),
            b16(BLK, BLK), b16(BLK, BLK), b16(OWN, HALF, 512), b16(OWN, HALF, 512),
            b16(768, HALF), b16(768, HALF), f32(OWN, 32, HALF), f32(OWN, 32, HALF),
            f32(NC, ND, HALF), f32(NC, ND, HALF), f32(ND, 8, HALF), f32(ND, 8, HALF),
            pltpu.SemaphoreType.DMA((10,)), pltpu.SemaphoreType.DMA((10,)), pltpu.SemaphoreType.DMA((3,)),
        ],
        compiler_params=pltpu.CompilerParams(
            collective_id=0, has_side_effects=True, vmem_limit_bytes=48 << 20),
    )(*[pltpu.with_memory_space_constraint(x, pltpu.HBM) for x in (projected, filters.T, cotangent)])
    parts = [pltpu.with_memory_space_constraint(x, pltpu.VMEM) for x in (mixed, proj_grad, filter_grad)]
    results = pl.pallas_call(
        write_out,
        out_shape=[jax.ShapeDtypeStruct(x.shape, x.dtype) for x in (mixed, proj_grad, filter_grad)],
        in_specs=[vmem] * 3,
        out_specs=[pl.BlockSpec(memory_space=pl.ANY)] * 3,
        scratch_shapes=[pltpu.SemaphoreType.DMA((3,))],
    )(*parts)
    return results[0], results[1], results[2].T


def solution(mesh):
    in_specs = (P(None, "dp", "ctx"), P(None, ("ctx", "dp")), P("dp", "ctx"))
    out_specs = (P("dp", "ctx"), P(None, "dp", "ctx"), P(None, ("ctx", "dp")))
    return jax.shard_map(
        on_device, mesh=mesh, in_specs=in_specs, out_specs=out_specs, check_vma=False
    )
```

```python
import functools

import jax
import jax.numpy as jnp
from jax import lax
from jax.experimental import pallas as pl
from jax.experimental.pallas import tpu as pltpu
from jax.sharding import PartitionSpec as P

MESH = pl.DeviceIdType.MESH
GROUP = 16
NC = 16
ND = 8
OWN = 2
BLK = 256
HALF = 128
F32 = jnp.float32
BF16 = jnp.bfloat16
NT = (((1,), (1,)), ((), ()))


def dot(left, right):
    return jnp.dot(left, right, preferred_element_type=F32)


def dot_nt(left, right):
    return lax.dot_general(left, right, NT, preferred_element_type=F32)


def split(value):
    high = value.astype(BF16)
    return high, (value - high.astype(F32)).astype(BF16)


def kernel(
    proj_in, filt_in, cot_in, mixed, pgrad, fgrad,
    proj, filt, cot, filt_rows,
    sp, sq, rp, rq, yb, zb, cv, pv,
    fs, fd, ft, fr, hx, r1h, r1l,
    xh, xl, pth, ptl, qh, ql, s1, s2, fo, fa, fb, fc,
    ssem, rsem, lsem,
):
    me = lax.axis_index("ctx")
    dp = lax.axis_index("dp")

    def ctx_peer(o):
        return lax.rem(me + o, NC)

    def dp_peer(o):
        return lax.rem(dp + o, ND)

    def ctx_copy(kind, o, src, dst):
        return pltpu.make_async_remote_copy(
            src_ref=src, dst_ref=dst, send_sem=ssem.at[kind], recv_sem=rsem.at[kind],
            device_id=(ctx_peer(o), dp), device_id_type=MESH)

    def dp_copy(kind, o, src, dst):
        return pltpu.make_async_remote_copy(
            src_ref=src, dst_ref=dst, send_sem=ssem.at[8 + kind], recv_sem=rsem.at[8 + kind],
            device_id=(me, dp_peer(o)), device_id_type=MESH)

    def p_copy(o):
        return ctx_copy(0, o, sp.at[ctx_peer(o)], rp.at[:, me])

    def q_copy(g, o):
        return ctx_copy(1 if g == 0 else 10, o, sq.at[ctx_peer(o), g], rq.at[g, me])

    def y_copy(g, o):
        return ctx_copy(2 + g, o, yb.at[g, ctx_peer(o)], cv.at[me, g])

    def z_copy(g, o):
        return ctx_copy(4 + g, o, zb.at[g, ctx_peer(o)], pv.at[me, g])

    def f_copy(o):
        return ctx_copy(6, o, ft.at[lax.div(ctx_peer(o), 2)], fr.at[me])

    def g_copy(o):
        return ctx_copy(7, o, fo.at[ctx_peer(o)], fa.at[me])

    def fd_copy(o):
        return dp_copy(0, o, fs.at[dp_peer(o)], fd.at[dp])

    def gd_copy(o):
        return dp_copy(1, o, fb.at[dp_peer(o)], fc.at[dp])

    totals = [
        rp.at[:, pl.ds(0, NC - 1)], rq.at[0, pl.ds(0, NC - 1)],
        cv.at[pl.ds(0, NC - 1), 0], cv.at[pl.ds(0, NC - 1), 1],
        pv.at[pl.ds(0, NC - 1), 0], pv.at[pl.ds(0, NC - 1), 1],
        fr.at[pl.ds(0, NC - 1)], fa.at[pl.ds(0, NC - 1)],
        fd.at[pl.ds(0, ND - 1)], fc.at[pl.ds(0, ND - 1)], rq.at[1, pl.ds(0, NC - 1)],
    ]

    def arrived(kind):
        pltpu.make_async_copy(totals[kind], totals[kind], rsem.at[kind]).wait()

    def sent(kind):
        pltpu.make_async_copy(totals[kind], totals[kind], ssem.at[kind]).wait()

    def over(n, body):
        @pl.loop(1, n)
        def _(o):
            body(o)

    barrier = pltpu.get_barrier_semaphore()
    for o in (6, 2, 5, 7, 1, 3, 4):
        pl.semaphore_signal(barrier, inc=1, device_id=(me, dp_peer(o)), device_id_type=MESH)
    for o in range(1, NC):
        pl.semaphore_signal(barrier, inc=1, device_id=(ctx_peer(o), dp), device_id_type=MESH)
    loads = [
        pltpu.make_async_copy(filt_in, filt, lsem.at[0]),
        pltpu.make_async_copy(proj_in.at[pl.ds(1, 2)], proj.at[pl.ds(1, 2)], lsem.at[1]),
        pltpu.make_async_copy(proj_in.at[0], proj.at[0], lsem.at[2]),
        pltpu.make_async_copy(cot_in, cot, lsem.at[3]),
    ]
    for load in loads:
        load.start()
    loads[0].wait()
    filt_rows[...] = filt[...].T
    fs[...] = jnp.concatenate(
        [filt_rows[pl.ds(q, 64, stride=4), :] for q in range(4)], axis=1
    ).reshape(ND, 8, HALF)

    def block(k):
        return pl.ds(pl.multiple_of(k * 32, 32), 32)

    def product(k):
        return proj[1, block(k), :].astype(F32) * proj[2, block(k), :].astype(F32)

    def conv_cot(k):
        return cot[block(k), :].astype(F32) * proj[0, block(k), :].astype(F32)

    def pieces(value):
        for g in range(OWN):
            for h in range(2):
                yield g, h, value[g * 16 : g * 16 + 16, h * HALF : (h + 1) * HALF]

    pl.semaphore_wait(barrier, NC + ND - 2)
    for o in (6, 2, 5, 7, 1, 3, 4):
        fd_copy(o).start()
    loads[1].wait()

    def give_product(o):
        k = ctx_peer(o)
        for g, h, piece in pieces(product(k)):
            sp[k, g, h] = piece
        p_copy(o).start()

    over(NC, give_product)
    fd[dp] = fs[dp]
    for g, h, piece in pieces(product(me)):
        rp[g, me, h] = piece
    loads[2].wait()
    loads[3].wait()
    for g, h, piece in pieces(conv_cot(me)):
        rq[g, me, h] = piece

    @pl.loop(0, NC, unroll=4)
    def _(k):
        for g, h, piece in pieces(conv_cot(k)):
            sq[k, g, h] = piece

    hx[...] = jnp.zeros_like(hx)
    qh[512:, :] = jnp.zeros((256, HALF), BF16)
    ql[512:, :] = jnp.zeros((256, HALF), BF16)
    fo[...] = jnp.zeros_like(fo)
    s2[...] = jnp.zeros_like(s2)
    arrived(8)
    for s in range(8):
        ft[s] = fd[:, s, :]
    for o in range(1, NC):
        f_copy(o).start()
    for g in range(OWN):
        over(NC, lambda o: q_copy(g, o).start())
    fr[me] = ft[lax.div(me, 2)]
    arrived(6)

    lane32 = lax.broadcasted_iota(jnp.int32, (32, HALF), 1)
    odd = lax.rem(me, 2)
    for g in range(OWN):
        total = jnp.zeros((32, HALF), F32)
        for j in range(4):
            part = jnp.concatenate([fr[k, j :: 4, :] for k in range(NC)], axis=0)
            turned = [pltpu.roll(part, (32 * (j - 2 * e - g)) % HALF, axis=1) for e in range(2)]
            part = jnp.where(odd == 1, turned[1], turned[0])
            total = jnp.where((lane32 >= 32 * j) & (lane32 < 32 * j + 32), part, total)
        hx[g, 8:40, :] = total

    row = lax.broadcasted_iota(jnp.int32, (HALF, HALF), 0)
    lane = lax.broadcasted_iota(jnp.int32, (HALF, HALF), 1)

    def build(g):
        for q in range(32):
            first = jnp.broadcast_to(hx[g, 39 - q : 40 - q, :], (HALF, HALF))
            second = jnp.broadcast_to(hx[g, 38 - q : 39 - q, :], (HALF, HALF))
            value = jnp.where(lane + row < HALF, first, second)
            high, low = split(pltpu.roll(value, 0, axis=1, stride=1, stride_axis=0))
            r1h[g, q * HALF : (q + 1) * HALF, :] = high
            r1l[g, q * HALF : (q + 1) * HALF, :] = low
        r1h[g, 32 * HALF :, :] = jnp.zeros((HALF, HALF), BF16)
        r1l[g, 32 * HALF :, :] = jnp.zeros((HALF, HALF), BF16)

    def tile(strip, g, d):
        start = 3968 - 256 * d
        return jnp.concatenate(
            [strip[g, start : start + BLK, :], strip[g, start - HALF : start - HALF + BLK, :]],
            axis=1)

    flip = (row + lane == HALF - 1).astype(BF16)

    arrived(0)
    @pl.loop(0, OWN)
    def _(g):
        build(g)
        whole = jnp.concatenate(
            [rp[g, :, 0].reshape(BLK, HALF), rp[g, :, 1].reshape(BLK, HALF)], axis=1)
        xh[...], xl[...] = split(whole)
        for d in range(NC):
            n = (NC - d) * 16
            high, low = tile(r1h, g, d), tile(r1l, g, d)
            both = dot(jnp.concatenate([xh[:n], xl[:n]], axis=0), high)
            value = both[:n] + both[n:] + dot(xh[:n], low)
            value = value.reshape(NC - d, 16, BLK)
            if d == 0:
                yb[g] = value
            else:
                yb[g, d:] += value
        over(NC, lambda o: y_copy(g, o).start())
        cv[me, g] = yb[g, me]

    @pl.loop(0, OWN)
    def _(g):
        part_h, part_l = split(rp[g].reshape(512, HALF))
        pth[g] = dot_nt(flip, part_h).astype(BF16)
        ptl[g] = dot_nt(flip, part_l).astype(BF16)

    below = lane <= row
    lane16 = lax.broadcasted_iota(jnp.int32, (32, HALF), 1)
    def lag_sums(g):
        qh[:512, :], ql[:512, :] = split(rq[g].reshape(512, HALF))
        for e in range(16):
            depth = 512 if e < 8 else 256
            high, low = [
                jnp.concatenate([b[32 * e : 32 * e + depth, :], b[32 * e + 16 : 32 * e + 16 + depth, :]], axis=1)
                for b in (qh, ql)]
            left_h, left_l = pth[g, :, :depth], ptl[g, :, :depth]
            value = dot(left_h, high) + dot(left_l, high) + dot(left_h, low)
            for h in range(2):
                lag = 2 * e + h
                turned = pltpu.roll(value[:, h * HALF : (h + 1) * HALF], 1, axis=1, stride=1, stride_axis=0)
                s1[g, lag : lag + 1, :] = jnp.sum(jnp.where(below, turned, 0.0), axis=0, keepdims=True)
                if lag:
                    s2[g, lag - 1 : lag, :] = jnp.sum(jnp.where(below, 0.0, turned), axis=0, keepdims=True)
    def correlate(g):
        whole = jnp.concatenate(
            [rq[g, :, 0].reshape(BLK, HALF), rq[g, :, 1].reshape(BLK, HALF)], axis=1)
        xh[...], xl[...] = split(whole)
        for d in range(NC):
            n = (NC - d) * 16
            high, low = tile(r1h, g, d), tile(r1l, g, d)
            both = dot_nt(jnp.concatenate([xh[d * 16 :], xl[d * 16 :]], axis=0), high)
            value = both[:n] + both[n:] + dot_nt(xh[d * 16 :], low)
            value = value.reshape(NC - d, 16, BLK)
            if d == 0:
                zb[g] = value
            else:
                zb[g, : NC - d] += value
        over(NC, lambda o: z_copy(g, o).start())
        pv[me, g] = zb[g, me]

    arrived(1)
    lag_sums(0)
    correlate(0)
    arrived(10)
    lag_sums(1)
    sums = [s1[g] + s2[g] for g in range(OWN)]
    for j in range(4):
        total = jnp.zeros((32, HALF), F32)
        for g in range(OWN):
            for e in range(2):
                turned = pltpu.roll(sums[g], (32 * (2 * e + g - j)) % HALF, axis=1)
                start = 32 * (2 * e + g)
                mask = (lane16 >= start) & (lane16 < start + 32) & (odd == e)
                total = jnp.where(mask, turned, total)
        total = total.reshape(NC, 2, HALF)
        for h in range(2):
            fo[:, 4 * h + j, :] = total[:, h, :]
    for o in range(1, NC):
        g_copy(o).start()
    fa[me] = fo[me]

    correlate(1)

    arrived(7)
    for s in range(8):
        fb[:, s, :] = fa[2 * s] + fa[2 * s + 1]
    for o in (6, 2, 5, 7, 1, 3, 4):
        gd_copy(o).start()
    fc[dp] = fb[dp]

    arrived(2)
    arrived(3)

    @pl.loop(0, NC, unroll=4)
    def _(k):
        rows = pl.ds(pl.multiple_of(k * 32, 32), 32)
        conv = cv[k].reshape(32, BLK)
        mixed[rows, :] = (proj[0, rows, :].astype(F32) * conv).astype(BF16)
        pgrad[0, rows, :] = (cot[rows, :].astype(F32) * conv).astype(BF16)

    for g in range(OWN):
        arrived(4 + g)

        @pl.loop(0, NC, unroll=4)
        def _(k):
            rows = pl.ds(pl.multiple_of(k * 32 + g * 16, 16), 16)
            grad = pv[k, g]
            pgrad[1, rows, :] = (grad * proj[2, rows, :].astype(F32)).astype(BF16)
            pgrad[2, rows, :] = (grad * proj[1, rows, :].astype(F32)).astype(BF16)

    arrived(9)
    last = fc[...].reshape(64, HALF)
    for q in range(4):
        filt_rows[pl.ds(q, 64, stride=4), :] = last[:, 32 * q : 32 * q + 32]
    fgrad[...] = filt_rows[...].T

    for kind in range(11):
        sent(kind)


def write_out(mixed, pgrad, fgrad, mixed_out, pgrad_out, fgrad_out, sem):
    pairs = [(mixed, mixed_out), (pgrad, pgrad_out), (fgrad, fgrad_out)]
    copies = [pltpu.make_async_copy(a, b, sem.at[i]) for i, (a, b) in enumerate(pairs)]
    for copy in copies:
        copy.start()
    for copy in copies:
        copy.wait()


def on_device(projected, filters, cotangent):
    rows, cols = cotangent.shape
    vmem = pl.BlockSpec(memory_space=pltpu.VMEM)
    f32 = lambda *shape: pltpu.VMEM(shape, F32)
    b16 = lambda *shape: pltpu.VMEM(shape, BF16)
    strip = (OWN, 33 * HALF, HALF)
    whole = pl.BlockSpec(memory_space=pltpu.HBM)
    mixed, proj_grad, filter_grad = pl.pallas_call(
        kernel,
        out_shape=(
            jax.ShapeDtypeStruct((rows, cols), BF16),
            jax.ShapeDtypeStruct((3, rows, cols), BF16),
            jax.ShapeDtypeStruct(filters.shape[::-1], F32),
        ),
        in_specs=[whole] * 3,
        out_specs=(vmem,) * 3,
        scratch_shapes=[
            b16(3, rows, cols), f32(*filters.shape[::-1]), b16(rows, cols), f32(*filters.shape),
            f32(NC, OWN, 2, GROUP, HALF), f32(NC, OWN, 2, GROUP, HALF),
            f32(OWN, NC, 2, GROUP, HALF), f32(OWN, NC, 2, GROUP, HALF),
            f32(OWN, NC, GROUP, BLK), f32(OWN, NC, GROUP, BLK),
            f32(NC, OWN, GROUP, BLK), f32(NC, OWN, GROUP, BLK),
            f32(ND, 8, HALF), f32(ND, 8, HALF), f32(8, ND, HALF), f32(NC, 8, HALF),
            f32(OWN, 40, HALF), b16(*strip), b16(*strip),
            b16(BLK, BLK), b16(BLK, BLK), b16(OWN, HALF, 512), b16(OWN, HALF, 512),
            b16(768, HALF), b16(768, HALF), f32(OWN, 32, HALF), f32(OWN, 32, HALF),
            f32(NC, ND, HALF), f32(NC, ND, HALF), f32(ND, 8, HALF), f32(ND, 8, HALF),
            pltpu.SemaphoreType.DMA((11,)), pltpu.SemaphoreType.DMA((11,)), pltpu.SemaphoreType.DMA((4,)),
        ],
        compiler_params=pltpu.CompilerParams(
            collective_id=0, has_side_effects=True, vmem_limit_bytes=48 << 20),
    )(*[pltpu.with_memory_space_constraint(x, pltpu.HBM) for x in (projected, filters.T, cotangent)])
    parts = [pltpu.with_memory_space_constraint(x, pltpu.VMEM) for x in (mixed, proj_grad, filter_grad)]
    results = pl.pallas_call(
        write_out,
        out_shape=[jax.ShapeDtypeStruct(x.shape, x.dtype) for x in (mixed, proj_grad, filter_grad)],
        in_specs=[vmem] * 3,
        out_specs=[pl.BlockSpec(memory_space=pl.ANY)] * 3,
        scratch_shapes=[pltpu.SemaphoreType.DMA((3,))],
    )(*parts)
    return results[0], results[1], results[2].T


def solution(mesh):
    in_specs = (P(None, "dp", "ctx"), P(None, ("ctx", "dp")), P("dp", "ctx"))
    out_specs = (P("dp", "ctx"), P(None, "dp", "ctx"), P(None, ("ctx", "dp")))
    return jax.shard_map(
        on_device, mesh=mesh, in_specs=in_specs, out_specs=out_specs, check_vma=False
    )
```

```python
import functools

import jax
import jax.numpy as jnp
from jax import lax
from jax.experimental import pallas as pl
from jax.experimental.pallas import tpu as pltpu
from jax.sharding import PartitionSpec as P

MESH = pl.DeviceIdType.MESH
GROUP = 16
NC = 16
ND = 8
OWN = 2
BLK = 256
HALF = 128
F32 = jnp.float32
BF16 = jnp.bfloat16
NT = (((1,), (1,)), ((), ()))


def dot(left, right):
    return jnp.dot(left, right, preferred_element_type=F32)


def dot_nt(left, right):
    return lax.dot_general(left, right, NT, preferred_element_type=F32)


def split(value):
    high = value.astype(BF16)
    return high, (value - high.astype(F32)).astype(BF16)


def kernel(
    proj_in, filt_in, cot_in, mixed, pgrad, fgrad,
    proj, filt, cot, filt_rows,
    sp, sq, rp, rq, yb, zb, cv, pv,
    fs, fd, ft, fr, hx, r1h, r1l,
    xh, xl, pth, ptl, qh, ql, s1, s2, fo, fa, fb, fc,
    ssem, rsem, lsem,
):
    me = lax.axis_index("ctx")
    dp = lax.axis_index("dp")

    def ctx_peer(o):
        return lax.rem(me + o, NC)

    def dp_peer(o):
        return lax.rem(dp + o, ND)

    def ctx_copy(kind, o, src, dst):
        return pltpu.make_async_remote_copy(
            src_ref=src, dst_ref=dst, send_sem=ssem.at[kind], recv_sem=rsem.at[kind],
            device_id=(ctx_peer(o), dp), device_id_type=MESH)

    def dp_copy(kind, o, src, dst):
        return pltpu.make_async_remote_copy(
            src_ref=src, dst_ref=dst, send_sem=ssem.at[8 + kind], recv_sem=rsem.at[8 + kind],
            device_id=(me, dp_peer(o)), device_id_type=MESH)

    def p_copy(o):
        return ctx_copy(0, o, sp.at[ctx_peer(o)], rp.at[:, me])

    def q_copy(g, o):
        return ctx_copy(1 if g == 0 else 10, o, sq.at[ctx_peer(o), g], rq.at[g, me])

    def y_copy(g, o):
        return ctx_copy(2 + g, o, yb.at[g, ctx_peer(o)], cv.at[me, g])

    def z_copy(g, o):
        return ctx_copy(4 + g, o, zb.at[g, ctx_peer(o)], pv.at[me, g])

    def f_copy(o):
        return ctx_copy(6, o, ft.at[lax.div(ctx_peer(o), 2)], fr.at[me])

    def g_copy(o):
        return ctx_copy(7, o, fo.at[ctx_peer(o)], fa.at[me])

    def fd_copy(o):
        return dp_copy(0, o, fs.at[dp_peer(o)], fd.at[dp])

    def gd_copy(o):
        return dp_copy(1, o, fb.at[dp_peer(o)], fc.at[dp])

    totals = [
        rp.at[:, pl.ds(0, NC - 1)], rq.at[0, pl.ds(0, NC - 1)],
        cv.at[pl.ds(0, NC - 1), 0], cv.at[pl.ds(0, NC - 1), 1],
        pv.at[pl.ds(0, NC - 1), 0], pv.at[pl.ds(0, NC - 1), 1],
        fr.at[pl.ds(0, NC - 1)], fa.at[pl.ds(0, NC - 1)],
        fd.at[pl.ds(0, ND - 1)], fc.at[pl.ds(0, ND - 1)], rq.at[1, pl.ds(0, NC - 1)],
    ]

    def arrived(kind):
        pltpu.make_async_copy(totals[kind], totals[kind], rsem.at[kind]).wait()

    def sent(kind):
        pltpu.make_async_copy(totals[kind], totals[kind], ssem.at[kind]).wait()

    def over(n, body):
        @pl.loop(1, n)
        def _(o):
            body(o)

    barrier = pltpu.get_barrier_semaphore()
    for o in (6, 2, 5, 7, 1, 3, 4):
        pl.semaphore_signal(barrier, inc=1, device_id=(me, dp_peer(o)), device_id_type=MESH)
    for o in range(1, NC):
        pl.semaphore_signal(barrier, inc=1, device_id=(ctx_peer(o), dp), device_id_type=MESH)
    loads = [
        pltpu.make_async_copy(filt_in, filt, lsem.at[0]),
        pltpu.make_async_copy(proj_in.at[pl.ds(1, 2)], proj.at[pl.ds(1, 2)], lsem.at[1]),
        pltpu.make_async_copy(proj_in.at[0], proj.at[0], lsem.at[2]),
        pltpu.make_async_copy(cot_in, cot, lsem.at[3]),
    ]
    for load in loads:
        load.start()
    loads[0].wait()
    filt_rows[...] = filt[...].T
    fs[...] = jnp.concatenate(
        [filt_rows[pl.ds(q, 64, stride=4), :] for q in range(4)], axis=1
    ).reshape(ND, 8, HALF)

    def block(k):
        return pl.ds(pl.multiple_of(k * 32, 32), 32)

    def product(k):
        return proj[1, block(k), :].astype(F32) * proj[2, block(k), :].astype(F32)

    def conv_cot(k):
        return cot[block(k), :].astype(F32) * proj[0, block(k), :].astype(F32)

    def pieces(value):
        for g in range(OWN):
            for h in range(2):
                yield g, h, value[g * 16 : g * 16 + 16, h * HALF : (h + 1) * HALF]

    loads[1].wait()

    @pl.loop(0, NC, unroll=4)
    def _(k):
        for g, h, piece in pieces(product(k)):
            sp[k, g, h] = piece

    pl.semaphore_wait(barrier, NC + ND - 2)
    for o in (6, 2, 5, 7, 1, 3, 4):
        fd_copy(o).start()
    over(NC, lambda o: p_copy(o).start())
    fd[dp] = fs[dp]
    for g, h, piece in pieces(product(me)):
        rp[g, me, h] = piece
    loads[2].wait()
    loads[3].wait()
    for g, h, piece in pieces(conv_cot(me)):
        rq[g, me, h] = piece

    @pl.loop(0, NC, unroll=4)
    def _(k):
        for g, h, piece in pieces(conv_cot(k)):
            sq[k, g, h] = piece

    hx[...] = jnp.zeros_like(hx)
    qh[512:, :] = jnp.zeros((256, HALF), BF16)
    ql[512:, :] = jnp.zeros((256, HALF), BF16)
    fo[...] = jnp.zeros_like(fo)
    s2[...] = jnp.zeros_like(s2)
    arrived(8)
    for s in range(8):
        ft[s] = fd[:, s, :]
    for o in range(1, NC):
        f_copy(o).start()
    for g in range(OWN):
        over(NC, lambda o: q_copy(g, o).start())
    fr[me] = ft[lax.div(me, 2)]
    arrived(6)

    lane32 = lax.broadcasted_iota(jnp.int32, (32, HALF), 1)
    odd = lax.rem(me, 2)
    for g in range(OWN):
        total = jnp.zeros((32, HALF), F32)
        for j in range(4):
            part = jnp.concatenate([fr[k, j :: 4, :] for k in range(NC)], axis=0)
            turned = [pltpu.roll(part, (32 * (j - 2 * e - g)) % HALF, axis=1) for e in range(2)]
            part = jnp.where(odd == 1, turned[1], turned[0])
            total = jnp.where((lane32 >= 32 * j) & (lane32 < 32 * j + 32), part, total)
        hx[g, 8:40, :] = total

    row = lax.broadcasted_iota(jnp.int32, (HALF, HALF), 0)
    lane = lax.broadcasted_iota(jnp.int32, (HALF, HALF), 1)

    def build(g):
        for q in range(32):
            first = jnp.broadcast_to(hx[g, 39 - q : 40 - q, :], (HALF, HALF))
            second = jnp.broadcast_to(hx[g, 38 - q : 39 - q, :], (HALF, HALF))
            value = jnp.where(lane + row < HALF, first, second)
            high, low = split(pltpu.roll(value, 0, axis=1, stride=1, stride_axis=0))
            r1h[g, q * HALF : (q + 1) * HALF, :] = high
            r1l[g, q * HALF : (q + 1) * HALF, :] = low
        r1h[g, 32 * HALF :, :] = jnp.zeros((HALF, HALF), BF16)
        r1l[g, 32 * HALF :, :] = jnp.zeros((HALF, HALF), BF16)

    def tile(strip, g, d):
        start = 3968 - 256 * d
        return jnp.concatenate(
            [strip[g, start : start + BLK, :], strip[g, start - HALF : start - HALF + BLK, :]],
            axis=1)

    flip = (row + lane == HALF - 1).astype(BF16)

    arrived(0)
    @pl.loop(0, OWN)
    def _(g):
        build(g)
        whole = jnp.concatenate(
            [rp[g, :, 0].reshape(BLK, HALF), rp[g, :, 1].reshape(BLK, HALF)], axis=1)
        xh[...], xl[...] = split(whole)
        for d in range(NC):
            n = (NC - d) * 16
            high, low = tile(r1h, g, d), tile(r1l, g, d)
            both = dot(jnp.concatenate([xh[:n], xl[:n]], axis=0), high)
            value = both[:n] + both[n:] + dot(xh[:n], low)
            value = value.reshape(NC - d, 16, BLK)
            if d == 0:
                yb[g] = value
            else:
                yb[g, d:] += value
        over(NC, lambda o: y_copy(g, o).start())
        cv[me, g] = yb[g, me]

    @pl.loop(0, OWN)
    def _(g):
        part_h, part_l = split(rp[g].reshape(512, HALF))
        pth[g] = dot_nt(flip, part_h).astype(BF16)
        ptl[g] = dot_nt(flip, part_l).astype(BF16)

    below = lane <= row
    lane16 = lax.broadcasted_iota(jnp.int32, (32, HALF), 1)
    def lag_sums(g):
        qh[:512, :], ql[:512, :] = split(rq[g].reshape(512, HALF))
        for e in range(16):
            depth = 512 if e < 8 else 256
            high, low = [
                jnp.concatenate([b[32 * e : 32 * e + depth, :], b[32 * e + 16 : 32 * e + 16 + depth, :]], axis=1)
                for b in (qh, ql)]
            left_h, left_l = pth[g, :, :depth], ptl[g, :, :depth]
            value = dot(left_h, high) + dot(left_l, high) + dot(left_h, low)
            for h in range(2):
                lag = 2 * e + h
                turned = pltpu.roll(value[:, h * HALF : (h + 1) * HALF], 1, axis=1, stride=1, stride_axis=0)
                s1[g, lag : lag + 1, :] = jnp.sum(jnp.where(below, turned, 0.0), axis=0, keepdims=True)
                if lag:
                    s2[g, lag - 1 : lag, :] = jnp.sum(jnp.where(below, 0.0, turned), axis=0, keepdims=True)
    def correlate(g):
        whole = jnp.concatenate(
            [rq[g, :, 0].reshape(BLK, HALF), rq[g, :, 1].reshape(BLK, HALF)], axis=1)
        xh[...], xl[...] = split(whole)
        for d in range(NC):
            n = (NC - d) * 16
            high, low = tile(r1h, g, d), tile(r1l, g, d)
            both = dot_nt(jnp.concatenate([xh[d * 16 :], xl[d * 16 :]], axis=0), high)
            value = both[:n] + both[n:] + dot_nt(xh[d * 16 :], low)
            value = value.reshape(NC - d, 16, BLK)
            if d == 0:
                zb[g] = value
            else:
                zb[g, : NC - d] += value
        over(NC, lambda o: z_copy(g, o).start())
        pv[me, g] = zb[g, me]

    arrived(1)
    lag_sums(0)
    correlate(0)
    arrived(10)
    lag_sums(1)
    sums = [s1[g] + s2[g] for g in range(OWN)]
    for j in range(4):
        total = jnp.zeros((32, HALF), F32)
        for g in range(OWN):
            for e in range(2):
                turned = pltpu.roll(sums[g], (32 * (2 * e + g - j)) % HALF, axis=1)
                start = 32 * (2 * e + g)
                mask = (lane16 >= start) & (lane16 < start + 32) & (odd == e)
                total = jnp.where(mask, turned, total)
        total = total.reshape(NC, 2, HALF)
        for h in range(2):
            fo[:, 4 * h + j, :] = total[:, h, :]
    for o in range(1, NC):
        g_copy(o).start()
    fa[me] = fo[me]

    correlate(1)

    arrived(7)
    for s in range(8):
        fb[:, s, :] = fa[2 * s] + fa[2 * s + 1]
    for o in (6, 2, 5, 7, 1, 3, 4):
        gd_copy(o).start()
    fc[dp] = fb[dp]

    arrived(2)
    arrived(3)

    @pl.loop(0, NC, unroll=4)
    def _(k):
        rows = pl.ds(pl.multiple_of(k * 32, 32), 32)
        conv = cv[k].reshape(32, BLK)
        mixed[rows, :] = (proj[0, rows, :].astype(F32) * conv).astype(BF16)
        pgrad[0, rows, :] = (cot[rows, :].astype(F32) * conv).astype(BF16)

    for g in range(OWN):
        arrived(4 + g)

        @pl.loop(0, NC, unroll=4)
        def _(k):
            rows = pl.ds(pl.multiple_of(k * 32 + g * 16, 16), 16)
            grad = pv[k, g]
            pgrad[1, rows, :] = (grad * proj[2, rows, :].astype(F32)).astype(BF16)
            pgrad[2, rows, :] = (grad * proj[1, rows, :].astype(F32)).astype(BF16)

    arrived(9)
    last = fc[...].reshape(64, HALF)
    for q in range(4):
        filt_rows[pl.ds(q, 64, stride=4), :] = last[:, 32 * q : 32 * q + 32]
    fgrad[...] = filt_rows[...].T

    for kind in range(11):
        sent(kind)


def write_out(mixed, pgrad, fgrad, mixed_out, pgrad_out, fgrad_out, sem):
    pairs = [(mixed, mixed_out), (pgrad, pgrad_out), (fgrad, fgrad_out)]
    copies = [pltpu.make_async_copy(a, b, sem.at[i]) for i, (a, b) in enumerate(pairs)]
    for copy in copies:
        copy.start()
    for copy in copies:
        copy.wait()


def on_device(projected, filters, cotangent):
    rows, cols = cotangent.shape
    vmem = pl.BlockSpec(memory_space=pltpu.VMEM)
    f32 = lambda *shape: pltpu.VMEM(shape, F32)
    b16 = lambda *shape: pltpu.VMEM(shape, BF16)
    strip = (OWN, 33 * HALF, HALF)
    whole = pl.BlockSpec(memory_space=pltpu.HBM)
    mixed, proj_grad, filter_grad = pl.pallas_call(
        kernel,
        out_shape=(
            jax.ShapeDtypeStruct((rows, cols), BF16),
            jax.ShapeDtypeStruct((3, rows, cols), BF16),
            jax.ShapeDtypeStruct(filters.shape[::-1], F32),
        ),
        in_specs=[whole] * 3,
        out_specs=(vmem,) * 3,
        scratch_shapes=[
            b16(3, rows, cols), f32(*filters.shape[::-1]), b16(rows, cols), f32(*filters.shape),
            f32(NC, OWN, 2, GROUP, HALF), f32(NC, OWN, 2, GROUP, HALF),
            f32(OWN, NC, 2, GROUP, HALF), f32(OWN, NC, 2, GROUP, HALF),
            f32(OWN, NC, GROUP, BLK), f32(OWN, NC, GROUP, BLK),
            f32(NC, OWN, GROUP, BLK), f32(NC, OWN, GROUP, BLK),
            f32(ND, 8, HALF), f32(ND, 8, HALF), f32(8, ND, HALF), f32(NC, 8, HALF),
            f32(OWN, 40, HALF), b16(*strip), b16(*strip),
            b16(BLK, BLK), b16(BLK, BLK), b16(OWN, HALF, 512), b16(OWN, HALF, 512),
            b16(768, HALF), b16(768, HALF), f32(OWN, 32, HALF), f32(OWN, 32, HALF),
            f32(NC, ND, HALF), f32(NC, ND, HALF), f32(ND, 8, HALF), f32(ND, 8, HALF),
            pltpu.SemaphoreType.DMA((11,)), pltpu.SemaphoreType.DMA((11,)), pltpu.SemaphoreType.DMA((4,)),
        ],
        compiler_params=pltpu.CompilerParams(
            collective_id=0, has_side_effects=True, vmem_limit_bytes=48 << 20),
    )(*[pltpu.with_memory_space_constraint(x, pltpu.HBM) for x in (projected, filters.T, cotangent)])
    parts = [pltpu.with_memory_space_constraint(x, pltpu.VMEM) for x in (mixed, proj_grad, filter_grad)]
    results = pl.pallas_call(
        write_out,
        out_shape=[jax.ShapeDtypeStruct(x.shape, x.dtype) for x in (mixed, proj_grad, filter_grad)],
        in_specs=[vmem] * 3,
        out_specs=[pl.BlockSpec(memory_space=pl.ANY)] * 3,
        scratch_shapes=[pltpu.SemaphoreType.DMA((3,))],
    )(*parts)
    return results[0], results[1], results[2].T


def solution(mesh):
    in_specs = (P(None, "dp", "ctx"), P(None, ("ctx", "dp")), P("dp", "ctx"))
    out_specs = (P("dp", "ctx"), P(None, "dp", "ctx"), P(None, ("ctx", "dp")))
    return jax.shard_map(
        on_device, mesh=mesh, in_specs=in_specs, out_specs=out_specs, check_vma=False
    )
```

```python
import functools

import jax
import jax.numpy as jnp
from jax import lax
from jax.experimental import pallas as pl
from jax.experimental.pallas import tpu as pltpu
from jax.sharding import PartitionSpec as P

MESH = pl.DeviceIdType.MESH
GROUP = 16
NC = 16
ND = 8
OWN = 2
BLK = 256
HALF = 128
F32 = jnp.float32
BF16 = jnp.bfloat16
NT = (((1,), (1,)), ((), ()))


def dot(left, right):
    return jnp.dot(left, right, preferred_element_type=F32)


def dot_nt(left, right):
    return lax.dot_general(left, right, NT, preferred_element_type=F32)


def split(value):
    high = value.astype(BF16)
    return high, (value - high.astype(F32)).astype(BF16)


def kernel(
    proj_in, filt_in, cot_in, mixed, pgrad, fgrad,
    proj, filt, cot, filt_rows,
    sp, sq, rp, rq, yb, zb, cv, pv,
    fs, fd, ft, fr, hx, r1h, r1l,
    xh, xl, pth, ptl, qh, ql, s1, s2, fo, fa, fb, fc,
    ssem, rsem, lsem,
):
    me = lax.axis_index("ctx")
    dp = lax.axis_index("dp")

    def ctx_peer(o):
        return lax.rem(me + o, NC)

    def dp_peer(o):
        return lax.rem(dp + o, ND)

    def ctx_copy(kind, o, src, dst):
        return pltpu.make_async_remote_copy(
            src_ref=src, dst_ref=dst, send_sem=ssem.at[kind], recv_sem=rsem.at[kind],
            device_id=(ctx_peer(o), dp), device_id_type=MESH)

    def dp_copy(kind, o, src, dst):
        return pltpu.make_async_remote_copy(
            src_ref=src, dst_ref=dst, send_sem=ssem.at[8 + kind], recv_sem=rsem.at[8 + kind],
            device_id=(me, dp_peer(o)), device_id_type=MESH)

    def p_copy(o):
        return ctx_copy(0, o, sp.at[ctx_peer(o)], rp.at[:, me])

    def q_copy(g, o):
        return ctx_copy(1 if g == 0 else 10, o, sq.at[ctx_peer(o), g], rq.at[g, me])

    def y_copy(g, o):
        return ctx_copy(2 + g, o, yb.at[g, ctx_peer(o)], cv.at[me, g])

    def z_copy(g, o):
        return ctx_copy(4 + g, o, zb.at[g, ctx_peer(o)], pv.at[me, g])

    def f_copy(o):
        return ctx_copy(6, o, ft.at[lax.div(ctx_peer(o), 2)], fr.at[me])

    def g_copy(o):
        return ctx_copy(7, o, fo.at[ctx_peer(o)], fa.at[me])

    def fd_copy(o):
        return dp_copy(0, o, fs.at[dp_peer(o)], fd.at[dp])

    def gd_copy(o):
        return dp_copy(1, o, fb.at[dp_peer(o)], fc.at[dp])

    totals = [
        rp.at[:, pl.ds(0, NC - 1)], rq.at[0, pl.ds(0, NC - 1)],
        cv.at[pl.ds(0, NC - 1), 0], cv.at[pl.ds(0, NC - 1), 1],
        pv.at[pl.ds(0, NC - 1), 0], pv.at[pl.ds(0, NC - 1), 1],
        fr.at[pl.ds(0, NC - 1)], fa.at[pl.ds(0, NC - 1)],
        fd.at[pl.ds(0, ND - 1)], fc.at[pl.ds(0, ND - 1)], rq.at[1, pl.ds(0, NC - 1)],
    ]

    def arrived(kind):
        pltpu.make_async_copy(totals[kind], totals[kind], rsem.at[kind]).wait()

    def sent(kind):
        pltpu.make_async_copy(totals[kind], totals[kind], ssem.at[kind]).wait()

    def over(n, body):
        @pl.loop(1, n)
        def _(o):
            body(o)

    barrier = pltpu.get_barrier_semaphore()
    for o in (6, 2, 5, 7, 1, 3, 4):
        pl.semaphore_signal(barrier, inc=1, device_id=(me, dp_peer(o)), device_id_type=MESH)
    for o in range(1, NC):
        pl.semaphore_signal(barrier, inc=1, device_id=(ctx_peer(o), dp), device_id_type=MESH)
    loads = [
        pltpu.make_async_copy(filt_in, filt, lsem.at[0]),
        pltpu.make_async_copy(proj_in.at[pl.ds(1, 2)], proj.at[pl.ds(1, 2)], lsem.at[1]),
        pltpu.make_async_copy(proj_in.at[0], proj.at[0], lsem.at[2]),
        pltpu.make_async_copy(cot_in, cot, lsem.at[3]),
    ]
    for load in loads:
        load.start()
    loads[0].wait()
    filt_rows[...] = filt[...].T
    fs[...] = jnp.concatenate(
        [filt_rows[pl.ds(q, 64, stride=4), :] for q in range(4)], axis=1
    ).reshape(ND, 8, HALF)

    def block(k):
        return pl.ds(pl.multiple_of(k * 32, 32), 32)

    def product(k):
        return proj[1, block(k), :].astype(F32) * proj[2, block(k), :].astype(F32)

    def conv_cot(k):
        return cot[block(k), :].astype(F32) * proj[0, block(k), :].astype(F32)

    def pieces(value):
        for g in range(OWN):
            for h in range(2):
                yield g, h, value[g * 16 : g * 16 + 16, h * HALF : (h + 1) * HALF]

    loads[1].wait()

    @pl.loop(0, NC, unroll=4)
    def _(k):
        for g, h, piece in pieces(product(k)):
            sp[k, g, h] = piece

    pl.semaphore_wait(barrier, NC + ND - 2)
    for o in (6, 2, 5, 7, 1, 3, 4):
        fd_copy(o).start()
    for o in (10, 6, 8, 9, 7, 11, 5, 12, 4, 13, 3, 14, 2, 15, 1):
        p_copy(o).start()
    fd[dp] = fs[dp]
    for g, h, piece in pieces(product(me)):
        rp[g, me, h] = piece
    loads[2].wait()
    loads[3].wait()
    for g, h, piece in pieces(conv_cot(me)):
        rq[g, me, h] = piece

    @pl.loop(0, NC, unroll=4)
    def _(k):
        for g, h, piece in pieces(conv_cot(k)):
            sq[k, g, h] = piece

    hx[...] = jnp.zeros_like(hx)
    qh[512:, :] = jnp.zeros((256, HALF), BF16)
    ql[512:, :] = jnp.zeros((256, HALF), BF16)
    fo[...] = jnp.zeros_like(fo)
    s2[...] = jnp.zeros_like(s2)
    arrived(8)
    for s in range(8):
        ft[s] = fd[:, s, :]
    for o in (10, 6, 8, 9, 7, 11, 5, 12, 4, 13, 3, 14, 2, 15, 1):
        f_copy(o).start()
    for g in range(OWN):
        for o in (10, 6, 8, 9, 7, 11, 5, 12, 4, 13, 3, 14, 2, 15, 1):
            q_copy(g, o).start()
    fr[me] = ft[lax.div(me, 2)]
    arrived(6)

    lane32 = lax.broadcasted_iota(jnp.int32, (32, HALF), 1)
    odd = lax.rem(me, 2)
    for g in range(OWN):
        total = jnp.zeros((32, HALF), F32)
        for j in range(4):
            part = jnp.concatenate([fr[k, j :: 4, :] for k in range(NC)], axis=0)
            turned = [pltpu.roll(part, (32 * (j - 2 * e - g)) % HALF, axis=1) for e in range(2)]
            part = jnp.where(odd == 1, turned[1], turned[0])
            total = jnp.where((lane32 >= 32 * j) & (lane32 < 32 * j + 32), part, total)
        hx[g, 8:40, :] = total

    row = lax.broadcasted_iota(jnp.int32, (HALF, HALF), 0)
    lane = lax.broadcasted_iota(jnp.int32, (HALF, HALF), 1)

    def build(g):
        for q in range(32):
            first = jnp.broadcast_to(hx[g, 39 - q : 40 - q, :], (HALF, HALF))
            second = jnp.broadcast_to(hx[g, 38 - q : 39 - q, :], (HALF, HALF))
            value = jnp.where(lane + row < HALF, first, second)
            high, low = split(pltpu.roll(value, 0, axis=1, stride=1, stride_axis=0))
            r1h[g, q * HALF : (q + 1) * HALF, :] = high
            r1l[g, q * HALF : (q + 1) * HALF, :] = low
        r1h[g, 32 * HALF :, :] = jnp.zeros((HALF, HALF), BF16)
        r1l[g, 32 * HALF :, :] = jnp.zeros((HALF, HALF), BF16)

    def tile(strip, g, d):
        start = 3968 - 256 * d
        return jnp.concatenate(
            [strip[g, start : start + BLK, :], strip[g, start - HALF : start - HALF + BLK, :]],
            axis=1)

    flip = (row + lane == HALF - 1).astype(BF16)

    arrived(0)
    @pl.loop(0, OWN)
    def _(g):
        build(g)
        whole = jnp.concatenate(
            [rp[g, :, 0].reshape(BLK, HALF), rp[g, :, 1].reshape(BLK, HALF)], axis=1)
        xh[...], xl[...] = split(whole)
        for d in range(NC):
            n = (NC - d) * 16
            high, low = tile(r1h, g, d), tile(r1l, g, d)
            both = dot(jnp.concatenate([xh[:n], xl[:n]], axis=0), high)
            value = both[:n] + both[n:] + dot(xh[:n], low)
            value = value.reshape(NC - d, 16, BLK)
            if d == 0:
                yb[g] = value
            else:
                yb[g, d:] += value
        for o in (10, 6, 8, 9, 7, 11, 5, 12, 4, 13, 3, 14, 2, 15, 1):
            y_copy(g, o).start()
        cv[me, g] = yb[g, me]

    @pl.loop(0, OWN)
    def _(g):
        part_h, part_l = split(rp[g].reshape(512, HALF))
        pth[g] = dot_nt(flip, part_h).astype(BF16)
        ptl[g] = dot_nt(flip, part_l).astype(BF16)

    below = lane <= row
    lane16 = lax.broadcasted_iota(jnp.int32, (32, HALF), 1)
    def lag_sums(g):
        qh[:512, :], ql[:512, :] = split(rq[g].reshape(512, HALF))
        for e in range(16):
            depth = 512 if e < 8 else 256
            high, low = [
                jnp.concatenate([b[32 * e : 32 * e + depth, :], b[32 * e + 16 : 32 * e + 16 + depth, :]], axis=1)
                for b in (qh, ql)]
            left_h, left_l = pth[g, :, :depth], ptl[g, :, :depth]
            value = dot(left_h, high) + dot(left_l, high) + dot(left_h, low)
            for h in range(2):
                lag = 2 * e + h
                turned = pltpu.roll(value[:, h * HALF : (h + 1) * HALF], 1, axis=1, stride=1, stride_axis=0)
                s1[g, lag : lag + 1, :] = jnp.sum(jnp.where(below, turned, 0.0), axis=0, keepdims=True)
                if lag:
                    s2[g, lag - 1 : lag, :] = jnp.sum(jnp.where(below, 0.0, turned), axis=0, keepdims=True)
    def correlate(g):
        whole = jnp.concatenate(
            [rq[g, :, 0].reshape(BLK, HALF), rq[g, :, 1].reshape(BLK, HALF)], axis=1)
        xh[...], xl[...] = split(whole)
        for d in range(NC):
            n = (NC - d) * 16
            high, low = tile(r1h, g, d), tile(r1l, g, d)
            both = dot_nt(jnp.concatenate([xh[d * 16 :], xl[d * 16 :]], axis=0), high)
            value = both[:n] + both[n:] + dot_nt(xh[d * 16 :], low)
            value = value.reshape(NC - d, 16, BLK)
            if d == 0:
                zb[g] = value
            else:
                zb[g, : NC - d] += value
        for o in (10, 6, 8, 9, 7, 11, 5, 12, 4, 13, 3, 14, 2, 15, 1):
            z_copy(g, o).start()
        pv[me, g] = zb[g, me]

    arrived(1)
    lag_sums(0)
    correlate(0)
    arrived(10)
    lag_sums(1)
    sums = [s1[g] + s2[g] for g in range(OWN)]
    for j in range(4):
        total = jnp.zeros((32, HALF), F32)
        for g in range(OWN):
            for e in range(2):
                turned = pltpu.roll(sums[g], (32 * (2 * e + g - j)) % HALF, axis=1)
                start = 32 * (2 * e + g)
                mask = (lane16 >= start) & (lane16 < start + 32) & (odd == e)
                total = jnp.where(mask, turned, total)
        total = total.reshape(NC, 2, HALF)
        for h in range(2):
            fo[:, 4 * h + j, :] = total[:, h, :]
    for o in (10, 6, 8, 9, 7, 11, 5, 12, 4, 13, 3, 14, 2, 15, 1):
        g_copy(o).start()
    fa[me] = fo[me]

    correlate(1)

    arrived(7)
    for s in range(8):
        fb[:, s, :] = fa[2 * s] + fa[2 * s + 1]
    for o in (6, 2, 5, 7, 1, 3, 4):
        gd_copy(o).start()
    fc[dp] = fb[dp]

    arrived(2)
    arrived(3)

    @pl.loop(0, NC, unroll=4)
    def _(k):
        rows = pl.ds(pl.multiple_of(k * 32, 32), 32)
        conv = cv[k].reshape(32, BLK)
        mixed[rows, :] = (proj[0, rows, :].astype(F32) * conv).astype(BF16)
        pgrad[0, rows, :] = (cot[rows, :].astype(F32) * conv).astype(BF16)

    for g in range(OWN):
        arrived(4 + g)

        @pl.loop(0, NC, unroll=4)
        def _(k):
            rows = pl.ds(pl.multiple_of(k * 32 + g * 16, 16), 16)
            grad = pv[k, g]
            pgrad[1, rows, :] = (grad * proj[2, rows, :].astype(F32)).astype(BF16)
            pgrad[2, rows, :] = (grad * proj[1, rows, :].astype(F32)).astype(BF16)

    arrived(9)
    last = fc[...].reshape(64, HALF)
    for q in range(4):
        filt_rows[pl.ds(q, 64, stride=4), :] = last[:, 32 * q : 32 * q + 32]
    fgrad[...] = filt_rows[...].T

    for kind in range(11):
        sent(kind)


def write_out(mixed, pgrad, fgrad, mixed_out, pgrad_out, fgrad_out, sem):
    pairs = [(mixed, mixed_out), (pgrad, pgrad_out), (fgrad, fgrad_out)]
    copies = [pltpu.make_async_copy(a, b, sem.at[i]) for i, (a, b) in enumerate(pairs)]
    for copy in copies:
        copy.start()
    for copy in copies:
        copy.wait()


def on_device(projected, filters, cotangent):
    rows, cols = cotangent.shape
    vmem = pl.BlockSpec(memory_space=pltpu.VMEM)
    f32 = lambda *shape: pltpu.VMEM(shape, F32)
    b16 = lambda *shape: pltpu.VMEM(shape, BF16)
    strip = (OWN, 33 * HALF, HALF)
    whole = pl.BlockSpec(memory_space=pltpu.HBM)
    mixed, proj_grad, filter_grad = pl.pallas_call(
        kernel,
        out_shape=(
            jax.ShapeDtypeStruct((rows, cols), BF16),
            jax.ShapeDtypeStruct((3, rows, cols), BF16),
            jax.ShapeDtypeStruct(filters.shape[::-1], F32),
        ),
        in_specs=[whole] * 3,
        out_specs=(vmem,) * 3,
        scratch_shapes=[
            b16(3, rows, cols), f32(*filters.shape[::-1]), b16(rows, cols), f32(*filters.shape),
            f32(NC, OWN, 2, GROUP, HALF), f32(NC, OWN, 2, GROUP, HALF),
            f32(OWN, NC, 2, GROUP, HALF), f32(OWN, NC, 2, GROUP, HALF),
            f32(OWN, NC, GROUP, BLK), f32(OWN, NC, GROUP, BLK),
            f32(NC, OWN, GROUP, BLK), f32(NC, OWN, GROUP, BLK),
            f32(ND, 8, HALF), f32(ND, 8, HALF), f32(8, ND, HALF), f32(NC, 8, HALF),
            f32(OWN, 40, HALF), b16(*strip), b16(*strip),
            b16(BLK, BLK), b16(BLK, BLK), b16(OWN, HALF, 512), b16(OWN, HALF, 512),
            b16(768, HALF), b16(768, HALF), f32(OWN, 32, HALF), f32(OWN, 32, HALF),
            f32(NC, ND, HALF), f32(NC, ND, HALF), f32(ND, 8, HALF), f32(ND, 8, HALF),
            pltpu.SemaphoreType.DMA((11,)), pltpu.SemaphoreType.DMA((11,)), pltpu.SemaphoreType.DMA((4,)),
        ],
        compiler_params=pltpu.CompilerParams(
            collective_id=0, has_side_effects=True, vmem_limit_bytes=48 << 20),
    )(*[pltpu.with_memory_space_constraint(x, pltpu.HBM) for x in (projected, filters.T, cotangent)])
    parts = [pltpu.with_memory_space_constraint(x, pltpu.VMEM) for x in (mixed, proj_grad, filter_grad)]
    results = pl.pallas_call(
        write_out,
        out_shape=[jax.ShapeDtypeStruct(x.shape, x.dtype) for x in (mixed, proj_grad, filter_grad)],
        in_specs=[vmem] * 3,
        out_specs=[pl.BlockSpec(memory_space=pl.ANY)] * 3,
        scratch_shapes=[pltpu.SemaphoreType.DMA((3,))],
    )(*parts)
    return results[0], results[1], results[2].T


def solution(mesh):
    in_specs = (P(None, "dp", "ctx"), P(None, ("ctx", "dp")), P("dp", "ctx"))
    out_specs = (P("dp", "ctx"), P(None, "dp", "ctx"), P(None, ("ctx", "dp")))
    return jax.shard_map(
        on_device, mesh=mesh, in_specs=in_specs, out_specs=out_specs, check_vma=False
    )
```

```python
import functools

import jax
import jax.numpy as jnp
from jax import lax
from jax.experimental import pallas as pl
from jax.experimental.pallas import tpu as pltpu
from jax.sharding import PartitionSpec as P

MESH = pl.DeviceIdType.MESH
GROUP = 16
NC = 16
ND = 8
OWN = 2
BLK = 256
HALF = 128
F32 = jnp.float32
BF16 = jnp.bfloat16
NT = (((1,), (1,)), ((), ()))


def dot(left, right):
    return jnp.dot(left, right, preferred_element_type=F32)


def dot_nt(left, right):
    return lax.dot_general(left, right, NT, preferred_element_type=F32)


def split(value):
    high = value.astype(BF16)
    return high, (value - high.astype(F32)).astype(BF16)


def kernel(
    proj_in, filt_in, cot_in, mixed, pgrad, fgrad,
    proj, filt, cot, filt_rows,
    sp, sq, rp, rq, yb, zb, cv, pv,
    fs, fd, ft, fr, hx, r1h, r1l,
    xh, xl, pth, ptl, qh, ql, s1, s2, fo, fa, fb, fc,
    ssem, rsem, lsem,
):
    me = lax.axis_index("ctx")
    dp = lax.axis_index("dp")

    def ctx_peer(o):
        return lax.rem(me + o, NC)

    def dp_peer(o):
        return lax.rem(dp + o, ND)

    def ctx_copy(kind, o, src, dst):
        return pltpu.make_async_remote_copy(
            src_ref=src, dst_ref=dst, send_sem=ssem.at[kind], recv_sem=rsem.at[kind],
            device_id=(ctx_peer(o), dp), device_id_type=MESH)

    def dp_copy(kind, o, src, dst):
        return pltpu.make_async_remote_copy(
            src_ref=src, dst_ref=dst, send_sem=ssem.at[8 + kind], recv_sem=rsem.at[8 + kind],
            device_id=(me, dp_peer(o)), device_id_type=MESH)

    def p_copy(o):
        return ctx_copy(0, o, sp.at[ctx_peer(o)], rp.at[:, me])

    def q_copy(g, o):
        return ctx_copy(1 if g == 0 else 10, o, sq.at[ctx_peer(o), g], rq.at[g, me])

    def y_copy(g, o):
        return ctx_copy(2 + g, o, yb.at[g, ctx_peer(o)], cv.at[me, g])

    def z_copy(g, o):
        return ctx_copy(4 + g, o, zb.at[g, ctx_peer(o)], pv.at[me, g])

    def f_copy(o):
        return ctx_copy(6, o, ft.at[lax.div(ctx_peer(o), 2)], fr.at[me])

    def g_copy(o):
        return ctx_copy(7, o, fo.at[ctx_peer(o)], fa.at[me])

    def fd_copy(o):
        return dp_copy(0, o, fs.at[dp_peer(o)], fd.at[dp])

    def gd_copy(o):
        return dp_copy(1, o, fb.at[dp_peer(o)], fc.at[dp])

    totals = [
        rp.at[:, pl.ds(0, NC - 1)], rq.at[0, pl.ds(0, NC - 1)],
        cv.at[pl.ds(0, NC - 1), 0], cv.at[pl.ds(0, NC - 1), 1],
        pv.at[pl.ds(0, NC - 1), 0], pv.at[pl.ds(0, NC - 1), 1],
        fr.at[pl.ds(0, NC - 1)], fa.at[pl.ds(0, NC - 1)],
        fd.at[pl.ds(0, ND - 1)], fc.at[pl.ds(0, ND - 1)], rq.at[1, pl.ds(0, NC - 1)],
    ]

    def arrived(kind):
        pltpu.make_async_copy(totals[kind], totals[kind], rsem.at[kind]).wait()

    def sent(kind):
        pltpu.make_async_copy(totals[kind], totals[kind], ssem.at[kind]).wait()

    def over(n, body):
        @pl.loop(1, n)
        def _(o):
            body(o)

    barrier = pltpu.get_barrier_semaphore()
    for o in (6, 2, 5, 7, 1, 3, 4):
        pl.semaphore_signal(barrier, inc=1, device_id=(me, dp_peer(o)), device_id_type=MESH)
    for o in (10, 6, 8, 9, 7, 11, 5, 12, 4, 13, 3, 14, 2, 15, 1):
        pl.semaphore_signal(barrier, inc=1, device_id=(ctx_peer(o), dp), device_id_type=MESH)
    loads = [
        pltpu.make_async_copy(filt_in, filt, lsem.at[0]),
        pltpu.make_async_copy(proj_in.at[pl.ds(1, 2)], proj.at[pl.ds(1, 2)], lsem.at[1]),
        pltpu.make_async_copy(proj_in.at[0], proj.at[0], lsem.at[2]),
        pltpu.make_async_copy(cot_in, cot, lsem.at[3]),
    ]
    for load in loads:
        load.start()
    loads[0].wait()
    filt_rows[...] = filt[...].T
    fs[...] = jnp.concatenate(
        [filt_rows[pl.ds(q, 64, stride=4), :] for q in range(4)], axis=1
    ).reshape(ND, 8, HALF)

    def block(k):
        return pl.ds(pl.multiple_of(k * 32, 32), 32)

    def product(k):
        return proj[1, block(k), :].astype(F32) * proj[2, block(k), :].astype(F32)

    def conv_cot(k):
        return cot[block(k), :].astype(F32) * proj[0, block(k), :].astype(F32)

    def pieces(value):
        for g in range(OWN):
            for h in range(2):
                yield g, h, value[g * 16 : g * 16 + 16, h * HALF : (h + 1) * HALF]

    loads[1].wait()

    @pl.loop(0, NC, unroll=4)
    def _(k):
        for g, h, piece in pieces(product(k)):
            sp[k, g, h] = piece

    pl.semaphore_wait(barrier, NC + ND - 2)
    for o in (6, 2, 5, 7, 1, 3, 4):
        fd_copy(o).start()
    for o in (10, 6, 8, 9, 7, 11, 5, 12, 4, 13, 3, 14, 2, 15, 1):
        p_copy(o).start()
    fd[dp] = fs[dp]
    for g, h, piece in pieces(product(me)):
        rp[g, me, h] = piece
    loads[2].wait()
    loads[3].wait()
    for g, h, piece in pieces(conv_cot(me)):
        rq[g, me, h] = piece

    @pl.loop(0, NC, unroll=4)
    def _(k):
        for g, h, piece in pieces(conv_cot(k)):
            sq[k, g, h] = piece

    hx[...] = jnp.zeros_like(hx)
    qh[512:, :] = jnp.zeros((256, HALF), BF16)
    ql[512:, :] = jnp.zeros((256, HALF), BF16)
    fo[...] = jnp.zeros_like(fo)
    s2[...] = jnp.zeros_like(s2)
    arrived(8)
    for s in range(8):
        ft[s] = fd[:, s, :]
    for o in (10, 6, 8, 9, 7, 11, 5, 12, 4, 13, 3, 14, 2, 15, 1):
        f_copy(o).start()
    for g in range(OWN):
        for o in (10, 6, 8, 9, 7, 11, 5, 12, 4, 13, 3, 14, 2, 15, 1):
            q_copy(g, o).start()
    fr[me] = ft[lax.div(me, 2)]
    arrived(6)

    lane32 = lax.broadcasted_iota(jnp.int32, (32, HALF), 1)
    odd = lax.rem(me, 2)
    for g in range(OWN):
        total = jnp.zeros((32, HALF), F32)
        for j in range(4):
            part = jnp.concatenate([fr[k, j :: 4, :] for k in range(NC)], axis=0)
            turned = [pltpu.roll(part, (32 * (j - 2 * e - g)) % HALF, axis=1) for e in range(2)]
            part = jnp.where(odd == 1, turned[1], turned[0])
            total = jnp.where((lane32 >= 32 * j) & (lane32 < 32 * j + 32), part, total)
        hx[g, 8:40, :] = total

    row = lax.broadcasted_iota(jnp.int32, (HALF, HALF), 0)
    lane = lax.broadcasted_iota(jnp.int32, (HALF, HALF), 1)

    def build(g):
        for q in range(32):
            first = jnp.broadcast_to(hx[g, 39 - q : 40 - q, :], (HALF, HALF))
            second = jnp.broadcast_to(hx[g, 38 - q : 39 - q, :], (HALF, HALF))
            value = jnp.where(lane + row < HALF, first, second)
            high, low = split(pltpu.roll(value, 0, axis=1, stride=1, stride_axis=0))
            r1h[g, q * HALF : (q + 1) * HALF, :] = high
            r1l[g, q * HALF : (q + 1) * HALF, :] = low
        r1h[g, 32 * HALF :, :] = jnp.zeros((HALF, HALF), BF16)
        r1l[g, 32 * HALF :, :] = jnp.zeros((HALF, HALF), BF16)

    def tile(strip, g, d):
        start = 3968 - 256 * d
        return jnp.concatenate(
            [strip[g, start : start + BLK, :], strip[g, start - HALF : start - HALF + BLK, :]],
            axis=1)

    flip = (row + lane == HALF - 1).astype(BF16)

    arrived(0)
    @pl.loop(0, OWN)
    def _(g):
        build(g)
        whole = jnp.concatenate(
            [rp[g, :, 0].reshape(BLK, HALF), rp[g, :, 1].reshape(BLK, HALF)], axis=1)
        xh[...], xl[...] = split(whole)
        for d in range(NC):
            n = (NC - d) * 16
            high, low = tile(r1h, g, d), tile(r1l, g, d)
            both = dot(jnp.concatenate([xh[:n], xl[:n]], axis=0), high)
            value = both[:n] + both[n:] + dot(xh[:n], low)
            value = value.reshape(NC - d, 16, BLK)
            if d == 0:
                yb[g] = value
            else:
                yb[g, d:] += value
        for o in (10, 6, 8, 9, 7, 11, 5, 12, 4, 13, 3, 14, 2, 15, 1):
            y_copy(g, o).start()
        cv[me, g] = yb[g, me]

    @pl.loop(0, OWN)
    def _(g):
        part_h, part_l = split(rp[g].reshape(512, HALF))
        pth[g] = dot_nt(flip, part_h).astype(BF16)
        ptl[g] = dot_nt(flip, part_l).astype(BF16)

    below = lane <= row
    lane16 = lax.broadcasted_iota(jnp.int32, (32, HALF), 1)
    def lag_sums(g):
        qh[:512, :], ql[:512, :] = split(rq[g].reshape(512, HALF))
        for e in range(16):
            depth = 512 if e < 8 else 256
            high, low = [
                jnp.concatenate([b[32 * e : 32 * e + depth, :], b[32 * e + 16 : 32 * e + 16 + depth, :]], axis=1)
                for b in (qh, ql)]
            left_h, left_l = pth[g, :, :depth], ptl[g, :, :depth]
            value = dot(left_h, high) + dot(left_l, high) + dot(left_h, low)
            for h in range(2):
                lag = 2 * e + h
                turned = pltpu.roll(value[:, h * HALF : (h + 1) * HALF], 1, axis=1, stride=1, stride_axis=0)
                s1[g, lag : lag + 1, :] = jnp.sum(jnp.where(below, turned, 0.0), axis=0, keepdims=True)
                if lag:
                    s2[g, lag - 1 : lag, :] = jnp.sum(jnp.where(below, 0.0, turned), axis=0, keepdims=True)
    def correlate(g):
        whole = jnp.concatenate(
            [rq[g, :, 0].reshape(BLK, HALF), rq[g, :, 1].reshape(BLK, HALF)], axis=1)
        xh[...], xl[...] = split(whole)
        for d in range(NC):
            n = (NC - d) * 16
            high, low = tile(r1h, g, d), tile(r1l, g, d)
            both = dot_nt(jnp.concatenate([xh[d * 16 :], xl[d * 16 :]], axis=0), high)
            value = both[:n] + both[n:] + dot_nt(xh[d * 16 :], low)
            value = value.reshape(NC - d, 16, BLK)
            if d == 0:
                zb[g] = value
            else:
                zb[g, : NC - d] += value
        for o in (10, 6, 8, 9, 7, 11, 5, 12, 4, 13, 3, 14, 2, 15, 1):
            z_copy(g, o).start()
        pv[me, g] = zb[g, me]

    arrived(1)
    lag_sums(0)
    correlate(0)
    arrived(10)
    lag_sums(1)
    sums = [s1[g] + s2[g] for g in range(OWN)]
    for j in range(4):
        total = jnp.zeros((32, HALF), F32)
        for g in range(OWN):
            for e in range(2):
                turned = pltpu.roll(sums[g], (32 * (2 * e + g - j)) % HALF, axis=1)
                start = 32 * (2 * e + g)
                mask = (lane16 >= start) & (lane16 < start + 32) & (odd == e)
                total = jnp.where(mask, turned, total)
        total = total.reshape(NC, 2, HALF)
        for h in range(2):
            fo[:, 4 * h + j, :] = total[:, h, :]
    for o in (10, 6, 8, 9, 7, 11, 5, 12, 4, 13, 3, 14, 2, 15, 1):
        g_copy(o).start()
    fa[me] = fo[me]

    correlate(1)

    arrived(7)
    for s in range(8):
        fb[:, s, :] = fa[2 * s] + fa[2 * s + 1]
    for o in (6, 2, 5, 7, 1, 3, 4):
        gd_copy(o).start()
    fc[dp] = fb[dp]

    arrived(2)
    arrived(3)

    @pl.loop(0, NC, unroll=4)
    def _(k):
        rows = pl.ds(pl.multiple_of(k * 32, 32), 32)
        conv = cv[k].reshape(32, BLK)
        mixed[rows, :] = (proj[0, rows, :].astype(F32) * conv).astype(BF16)
        pgrad[0, rows, :] = (cot[rows, :].astype(F32) * conv).astype(BF16)

    for g in range(OWN):
        arrived(4 + g)

        @pl.loop(0, NC, unroll=4)
        def _(k):
            rows = pl.ds(pl.multiple_of(k * 32 + g * 16, 16), 16)
            grad = pv[k, g]
            pgrad[1, rows, :] = (grad * proj[2, rows, :].astype(F32)).astype(BF16)
            pgrad[2, rows, :] = (grad * proj[1, rows, :].astype(F32)).astype(BF16)

    arrived(9)
    last = fc[...].reshape(64, HALF)
    for q in range(4):
        filt_rows[pl.ds(q, 64, stride=4), :] = last[:, 32 * q : 32 * q + 32]
    fgrad[...] = filt_rows[...].T

    for kind in range(11):
        sent(kind)


def write_out(mixed, pgrad, fgrad, mixed_out, pgrad_out, fgrad_out, sem):
    pairs = [(mixed, mixed_out), (pgrad, pgrad_out), (fgrad, fgrad_out)]
    copies = [pltpu.make_async_copy(a, b, sem.at[i]) for i, (a, b) in enumerate(pairs)]
    for copy in copies:
        copy.start()
    for copy in copies:
        copy.wait()


def on_device(projected, filters, cotangent):
    rows, cols = cotangent.shape
    vmem = pl.BlockSpec(memory_space=pltpu.VMEM)
    f32 = lambda *shape: pltpu.VMEM(shape, F32)
    b16 = lambda *shape: pltpu.VMEM(shape, BF16)
    strip = (OWN, 33 * HALF, HALF)
    whole = pl.BlockSpec(memory_space=pltpu.HBM)
    mixed, proj_grad, filter_grad = pl.pallas_call(
        kernel,
        out_shape=(
            jax.ShapeDtypeStruct((rows, cols), BF16),
            jax.ShapeDtypeStruct((3, rows, cols), BF16),
            jax.ShapeDtypeStruct(filters.shape[::-1], F32),
        ),
        in_specs=[whole] * 3,
        out_specs=(vmem,) * 3,
        scratch_shapes=[
            b16(3, rows, cols), f32(*filters.shape[::-1]), b16(rows, cols), f32(*filters.shape),
            f32(NC, OWN, 2, GROUP, HALF), f32(NC, OWN, 2, GROUP, HALF),
            f32(OWN, NC, 2, GROUP, HALF), f32(OWN, NC, 2, GROUP, HALF),
            f32(OWN, NC, GROUP, BLK), f32(OWN, NC, GROUP, BLK),
            f32(NC, OWN, GROUP, BLK), f32(NC, OWN, GROUP, BLK),
            f32(ND, 8, HALF), f32(ND, 8, HALF), f32(8, ND, HALF), f32(NC, 8, HALF),
            f32(OWN, 40, HALF), b16(*strip), b16(*strip),
            b16(BLK, BLK), b16(BLK, BLK), b16(OWN, HALF, 512), b16(OWN, HALF, 512),
            b16(768, HALF), b16(768, HALF), f32(OWN, 32, HALF), f32(OWN, 32, HALF),
            f32(NC, ND, HALF), f32(NC, ND, HALF), f32(ND, 8, HALF), f32(ND, 8, HALF),
            pltpu.SemaphoreType.DMA((11,)), pltpu.SemaphoreType.DMA((11,)), pltpu.SemaphoreType.DMA((4,)),
        ],
        compiler_params=pltpu.CompilerParams(
            collective_id=0, has_side_effects=True, vmem_limit_bytes=48 << 20),
    )(*[pltpu.with_memory_space_constraint(x, pltpu.HBM) for x in (projected, filters.T, cotangent)])
    parts = [pltpu.with_memory_space_constraint(x, pltpu.VMEM) for x in (mixed, proj_grad, filter_grad)]
    results = pl.pallas_call(
        write_out,
        out_shape=[jax.ShapeDtypeStruct(x.shape, x.dtype) for x in (mixed, proj_grad, filter_grad)],
        in_specs=[vmem] * 3,
        out_specs=[pl.BlockSpec(memory_space=pl.ANY)] * 3,
        scratch_shapes=[pltpu.SemaphoreType.DMA((3,))],
    )(*parts)
    return results[0], results[1], results[2].T


def solution(mesh):
    in_specs = (P(None, "dp", "ctx"), P(None, ("ctx", "dp")), P("dp", "ctx"))
    out_specs = (P("dp", "ctx"), P(None, "dp", "ctx"), P(None, ("ctx", "dp")))
    return jax.shard_map(
        on_device, mesh=mesh, in_specs=in_specs, out_specs=out_specs, check_vma=False
    )
```
